32 devices in a mesh: grp: 4 (over y, x), dev: 8 (over z, core).
Axes of the slice: x: 2, y: 2, z: 4, core: 2. Of those that a mesh axis runs over, the one named last changes fastest.
Arguments:
- queries: bfloat16 [4096, 4096], P('dev', 'grp'), may hold values from -120 to 120
- keys: bfloat16 [4096, 512], P('dev', 'grp'), may hold values from -4.5 to 4.5
- values: bfloat16 [4096, 512], P('dev', 'grp'), may hold values from -6 to 6
- doc_ids: int32 [4096], replicated, may hold values from 0 to 15, never falling along the last dimension, each value on 1 to 2560 neighbouring positions
- out_weight: bfloat16 [4096, 2048], P('grp'), may hold values from -0.5 to 0.5
- norm_gain: float32 [2048], replicated, may hold values from 0.1 to 1.9
- expert_ids: int32 [8, 512, 8], P('dev', 'grp'), may hold values from 0 to 31, all different within a row; in each aligned block of 128 rows (0 to 127, 128 to 255, ..., all dimensions but the last counted through in order) at most 48 rows name the same one
- gate_values: float32 [8, 512, 8], P('dev', 'grp'), may hold values from 0.05 to 0.5
- expert_gate: bfloat16 [32, 2048, 768], P(('grp', 'dev')), may hold values from -0.125 to 0.125
- expert_up: bfloat16 [32, 2048, 768], P(('grp', 'dev')), may hold values from -0.125 to 0.125
- expert_down: bfloat16 [32, 768, 2048], P(('grp', 'dev')), may hold values from -0.21875 to 0.21875
Outputs:
- final: bfloat16 [8, 512, 2048], P('dev', 'grp')
The draws below stay inside these ranges and needn't reach their ends.
Inputs may be any that keep to these rules, and one draw needn't show every extreme that they name: doc_ids never fall along the tokens; every document has 1 to 2560 tokens and one has exactly 2560. `expert_ids`: each token names 8 different experts; among the 128 tokens of one device no expert is named by more than 48 tokens, and some expert reaches 48.
All inputs are finite; a program needn't handle non-finite values.
Results may differ from the reference program's by a relative error of at most 0.017.
Values may be sent and summed in bfloat16 or wider, within the bound.
No kernel may reach another device: no remote copies, remote signals or barrier semaphores. Data moves between devices by JAX's collectives and lax.ppermute only.
A program may use at most 128 MiB of HBM per device.

```python
import math
import jax
import jax.numpy as jnp
import numpy as np
from jax import lax

D = 2048
QUERY_HEAD_COUNT = 32
KEY_VALUE_HEADS = 4
HEAD_SIZE = 128
FF = 768
TOPK = 8
TOK_DEV = 128
DOCS = 16
EXPERTS = 32
ROWS_OWN = 512
TOKEN_TOTAL = 4096
DOC_MAX = 2560
CAP = 48
N_GRP = 4
N_DEV = 8


def attention_pair(key):
    folded_key = jax.random.fold_in(key, 101)
    key_portion, query_part = jax.random.split(folded_key, 2)
    every_key = jax.random.truncated_normal(key_portion, -4.5, 4.5, (TOKEN_TOTAL, KEY_VALUE_HEADS * HEAD_SIZE), jnp.float32)
    queries_all = jax.random.truncated_normal(query_part, -4.5, 4.5, (TOKEN_TOTAL, QUERY_HEAD_COUNT * HEAD_SIZE), jnp.float32)
    return (queries_all, every_key)


def draw_queries(key, part):
    return attention_pair(key)[0].astype(jnp.bfloat16)


def draw_keys(key, part):
    return attention_pair(key)[1].astype(jnp.bfloat16)


def level_of(stream_key, shape, cuts, low, high):
    factor_of = 1.0
    for position, parts in cuts:
        heights = jax.random.uniform(jax.random.fold_in(jax.random.fold_in(stream_key, 6), position), (parts,), jnp.float32, low / len(cuts), high / len(cuts))
        factor_of = factor_of * jnp.repeat(jnp.exp(heights), shape[position] // parts).reshape((-1,) + (1,) * (len(shape) - 1 - position))
    return factor_of


def profile(amount, total, most, slope):
    weights = [(1 << 20) // math.isqrt(standing ** slope) + 1 for standing in range(2, amount + 1)]
    surplus, holding = total - most - (amount - 1), [1] * (amount - 1)
    while surplus > 0:
        free = [i for i in range(amount - 1) if holding[i] < most]
        whole, left = sum([weights[i] for i in free]), surplus
        for i in free:
            more = min(most - holding[i], max(1, left * weights[i] // whole), surplus)
            holding[i] = holding[i] + more
            surplus = surplus - more
    return np.array([most] + holding)


def uneven_parts(own_key, amount, total, bound, lean):
    if amount == 2:
        one = jax.random.randint(own_key, (), max(1, total - bound), min(bound, total - 1) + 1)
        return jnp.stack([one, total - one])
    sizes = jnp.asarray(profile(amount, total, bound, lean), jnp.int32)
    twos = (amount - 1) // 2
    giver, receiver = sizes[1:1 + 2 * twos:2], sizes[2:2 + 2 * twos:2]
    margin = jnp.minimum(giver - 1, bound - receiver)
    shifted = jax.random.randint(jax.random.fold_in(own_key, 1), (twos,), 0, 1 << 20) % (margin + 1)
    sizes = sizes.at[1:1 + 2 * twos:2].set(giver - shifted).at[2:2 + 2 * twos:2].set(receiver + shifted)
    return sizes[jax.random.permutation(jax.random.fold_in(own_key, 2), amount)]


def shared_out(stream_key, own, number, rows, amount, top, limit, skew):
    ranking = jax.random.permutation(stream_key, amount)
    heavy_load, usual = portions_of(amount, rows * top, limit, skew, True), portions_of(amount, rows * top, limit, skew, False)
    places = jnp.arange(amount)

    def named(lengths, turn):
        used = int((lengths > 0).sum())
        fixed = max(1, used // 4)
        moved = fixed + (places - fixed + turn * (used - fixed)) % max(1, amount - fixed)
        return jnp.zeros((amount,), jnp.int32).at[ranking[jnp.where(places < fixed, places, moved)]].set(jnp.asarray(lengths, jnp.int32))

    lengths = jnp.where(number % 4 == 0, named(heavy_load, number // 4), named(usual, number - number // 4 - 1))
    mixed = jax.random.permutation(jax.random.fold_in(own, 3), amount)
    giver, receiver = mixed[0:amount // 2 * 2:2], mixed[1:amount // 2 * 2:2]
    slack = jnp.minimum(lengths[giver] - 1, limit - lengths[receiver]) // 2
    slack = jnp.where((giver == ranking[0]) | (receiver == ranking[0]) | (lengths[receiver] == 0), 0, jnp.maximum(slack, 0))
    moved = jax.random.randint(jax.random.fold_in(own, 4), (amount // 2,), 0, 1 << 20) % (slack + 1)
    lengths = lengths.at[giver].add(-moved).at[receiver].add(moved)
    members = jnp.searchsorted(jnp.cumsum(lengths), jnp.arange(rows * top), side="right").astype(jnp.int32)
    table = members.reshape(top, rows).T
    table = table[jax.random.permutation(jax.random.fold_in(own, 1), rows)]
    turn = jax.random.randint(jax.random.fold_in(own, 2), (rows, 1), 0, top)
    return jnp.take_along_axis(table, (jnp.arange(top)[None, :] + turn) % top, axis=1)


def portions_of(number_of, total, reach, slope, full):
    loads = [(1 << 20) // math.isqrt(standing ** slope) + 1 for standing in range(1, number_of + 1)]
    largest = reach if full else min(reach, max(-(-total // number_of), total * loads[0] // sum(loads)))
    least = 1 if total - largest >= number_of - 1 else 0
    counts, rest = [largest] + [least] * (number_of - 1), total - largest - least * (number_of - 1)
    while rest > 0:
        free = [i for i in range(1, number_of) if counts[i] < largest] or [i for i in range(1, number_of) if counts[i] < reach]
        mass, remaining = sum([loads[i] for i in free]), rest
        for i in free:
            extra = min(reach - counts[i], max(1, remaining * loads[i] // mass), rest)
            counts[i] = counts[i] + extra
            rest = rest - extra
    return np.array(counts)


def gaussian(key, dims, deviation, limit, cuts=(), kind=jnp.bfloat16):
    factor_of = level_of(key, dims, cuts, -0.22, 0.18) if cuts else 1.0
    values = jax.random.normal(key, dims, jnp.float32) * deviation * factor_of
    return jnp.minimum(jnp.maximum(values, -limit), limit).astype(kind)


def setup_inputs(seed: int = 0) -> dict:
    arg_keys = jax.random.split(jax.random.key(seed), 12)
    queries = draw_queries(jax.random.fold_in(arg_keys[11], 71), 0)
    keys = draw_keys(jax.random.fold_in(arg_keys[11], 71), 0)
    values = gaussian(arg_keys[2], (TOKEN_TOTAL, KEY_VALUE_HEADS * HEAD_SIZE), 1.0, 6.0, ((0, 8), (1, 4)))
    doc_ids = jnp.searchsorted(jnp.cumsum(uneven_parts(arg_keys[3], DOCS, TOKEN_TOTAL, DOC_MAX, 2)), jnp.arange(TOKEN_TOTAL), side="right").astype(jnp.int32)
    out_weight = gaussian(arg_keys[4], (QUERY_HEAD_COUNT * HEAD_SIZE, D), HEAD_SIZE ** -0.5, 0.5, ((0, 4),))
    norm_gain = jnp.clip(1.0 + 0.18 * jax.random.normal(arg_keys[5], (D,), jnp.float32), 0.1, 1.9)
    expert_ids_keys = jax.random.split(jax.random.fold_in(arg_keys[6], 1), N_DEV * ROWS_OWN // TOK_DEV)
    expert_ids_turns = jax.random.permutation(jax.random.fold_in(arg_keys[6], 3), N_DEV * ROWS_OWN // TOK_DEV)
    expert_ids = jax.vmap(lambda own, number: shared_out(jax.random.fold_in(arg_keys[6], 2), own, number, TOK_DEV, EXPERTS, TOPK, CAP, 2))(expert_ids_keys, expert_ids_turns).reshape((N_DEV, ROWS_OWN, TOPK))
    gate_values = jnp.clip(jnp.exp(math.log(0.5) - 2.3025851 * jax.random.uniform(arg_keys[7], (N_DEV, ROWS_OWN, TOPK), jnp.float32) ** level_of(arg_keys[7], (N_DEV, ROWS_OWN, TOPK), ((0, 8), (1, 4)), -0.2, 0.2)), 0.05, 0.5)
    expert_gate = gaussian(arg_keys[8], (EXPERTS, D, FF), D ** -0.5, 0.125, ((0, 32),))
    expert_up = gaussian(arg_keys[9], (EXPERTS, D, FF), D ** -0.5, 0.125, ((0, 32),))
    expert_down = gaussian(arg_keys[10], (EXPERTS, FF, D), FF ** -0.5, 0.21875, ((0, 32),))
    return dict(queries=queries, keys=keys, values=values, doc_ids=doc_ids, out_weight=out_weight, norm_gain=norm_gain, expert_ids=expert_ids, gate_values=gate_values, expert_gate=expert_gate, expert_up=expert_up, expert_down=expert_down)


def attend(queries, keys, values, doc_ids):
    block_row_count = min(512, TOKEN_TOTAL)
    sliding_span = min(DOC_MAX + block_row_count, TOKEN_TOTAL)
    shared_heads = QUERY_HEAD_COUNT // KEY_VALUE_HEADS
    scaling = 1.0 / math.sqrt(HEAD_SIZE)

    def one_block(block_index):
        row_offset = (block_index * block_row_count).astype(jnp.int32)
        key_offset = jnp.clip(row_offset + block_row_count - sliding_span, 0, TOKEN_TOTAL - sliding_span).astype(jnp.int32)
        query_row_slice = lax.dynamic_slice_in_dim(queries, row_offset, block_row_count, 0).astype(jnp.float32).reshape(block_row_count, KEY_VALUE_HEADS, shared_heads, HEAD_SIZE)
        key_row_slice = lax.dynamic_slice_in_dim(keys, key_offset, sliding_span, 0).astype(jnp.float32).reshape(sliding_span, KEY_VALUE_HEADS, HEAD_SIZE)
        value_row_slice = lax.dynamic_slice_in_dim(values, key_offset, sliding_span, 0).astype(jnp.float32).reshape(sliding_span, KEY_VALUE_HEADS, HEAD_SIZE)
        query_pos = row_offset + jnp.arange(block_row_count, dtype=jnp.int32)
        key_pos = key_offset + jnp.arange(sliding_span, dtype=jnp.int32)
        query_doc = lax.dynamic_slice_in_dim(doc_ids, row_offset, block_row_count, 0)
        key_doc = lax.dynamic_slice_in_dim(doc_ids, key_offset, sliding_span, 0)
        allowed = (query_doc[:, None] == key_doc[None, :]) & (key_pos[None, :] <= query_pos[:, None])
        scores = jnp.einsum('qngd,knd->ngqk', query_row_slice, key_row_slice) * scaling
        scores = jnp.where(allowed, scores, -jnp.inf)
        maxima = lax.optimization_barrier(jnp.max(scores, axis=-1, keepdims=True))
        weights = jnp.where(allowed, jnp.exp(scores - maxima), 0.0)
        totals = lax.optimization_barrier(jnp.sum(weights, axis=-1))
        rounded = lax.optimization_barrier(weights.astype(jnp.bfloat16))
        summed = jnp.einsum('ngqk,knd->ngqd', rounded.astype(jnp.float32), value_row_slice)
        result = summed / totals[..., None]
        return result.transpose(2, 0, 1, 3).reshape(block_row_count, QUERY_HEAD_COUNT * HEAD_SIZE).astype(jnp.bfloat16)
    blocks = lax.map(one_block, jnp.arange(TOKEN_TOTAL // block_row_count, dtype=jnp.int32))
    return blocks.reshape(TOKEN_TOTAL, QUERY_HEAD_COUNT * HEAD_SIZE)

def experts_apply(normed, routed_ids, gate_rows, expert_gate, expert_up, expert_down):
    row_limit = CAP * N_GRP * N_DEV

    def one_expert(summed, expert_index):
        matches = routed_ids == expert_index
        weight = lax.optimization_barrier(jnp.sum(jnp.where(matches, gate_rows, 0.0), axis=1))
        chosen = jnp.any(matches, axis=1)
        ordering = jnp.argsort(jnp.where(chosen, 0, 1).astype(jnp.int32), stable=True)[:row_limit].astype(jnp.int32)
        picked = normed[ordering]
        gate_act = jnp.dot(picked, expert_gate[expert_index], preferred_element_type=jnp.float32)
        up_act = jnp.dot(picked, expert_up[expert_index], preferred_element_type=jnp.float32)
        hidden = (jax.nn.silu(gate_act) * up_act).astype(jnp.bfloat16)
        expert_out = jnp.dot(hidden, expert_down[expert_index], preferred_element_type=jnp.float32).astype(jnp.bfloat16)
        summed = summed.at[ordering].add(weight[ordering][:, None] * expert_out.astype(jnp.float32))
        return (summed, None)
    start_sum = jnp.zeros((TOKEN_TOTAL, D), jnp.float32)
    summed, unused = lax.scan(one_expert, start_sum, jnp.arange(EXPERTS, dtype=jnp.int32))
    return summed

def reference(queries, keys, values, doc_ids, out_weight, norm_gain, expert_ids, gate_values, expert_gate, expert_up, expert_down):
    attended = attend(queries, keys, values, doc_ids)
    projected = jnp.dot(attended, out_weight, preferred_element_type=jnp.float32)
    normed = (projected * lax.rsqrt(lax.optimization_barrier(jnp.mean(projected * projected, axis=-1, keepdims=True)) + 1e-06) * norm_gain).astype(jnp.bfloat16)
    routed_ids = expert_ids.reshape(TOKEN_TOTAL, TOPK)
    gate_rows = gate_values.reshape(TOKEN_TOTAL, TOPK)
    mixed = experts_apply(normed, routed_ids, gate_rows, expert_gate, expert_up, expert_down)
    final = (projected + mixed).astype(jnp.bfloat16)
    return final.reshape(N_DEV, TOKEN_TOTAL // N_DEV, D)
```

```python
import functools
import math

import jax
import jax.numpy as jnp
from jax import lax
from jax.experimental import pallas as pl
from jax.experimental.pallas import tpu as pltpu
from jax.sharding import PartitionSpec as P

HEAD_SIZE = 128
KEY_BLOCK = 256
FF_TILE = 256
VMEM_BYTES = 56 * 1024 * 1024
LOW = -1e30


def after(value, *others):
    return lax.optimization_barrier((value, *others))[0]


def swap_x(value):
    return lax.ppermute(value, "grp", [(i, i ^ 1) for i in range(lax.axis_size("grp"))])


def swap_y(value):
    return lax.ppermute(value, "grp", [(i, i ^ 2) for i in range(lax.axis_size("grp"))])


def swap_core(value):
    return lax.ppermute(value, "dev", [(i, i ^ 1) for i in range(lax.axis_size("dev"))])


def turn(value, planes):
    count = lax.axis_size("dev")
    return lax.ppermute(value, "dev", [(i, (i - 2 * planes) % count) for i in range(count)])


def earlier(value, steps, sources=lambda source: True):
    count = lax.axis_size("dev")
    pairs = [(i, i + steps) for i in range(count - steps) if sources(i)]
    return lax.ppermute(value, "dev", pairs)


def gather_keys(keys, values, reach):
    core = lax.axis_index("dev") % 2
    own = jnp.concatenate([keys, values], axis=1)
    whole = reach // 2
    lanes = [own] + [earlier(own, 2 * j) for j in range(1, whole + 1)]
    others = [swap_core(lane) for lane in lanes]
    pieces = []
    for j in range(whole + 1):
        first = jnp.where(core == 0, lanes[j], others[j])
        second = jnp.where(core == 0, others[j], lanes[j])
        pieces = [first, second] + pieces
    if reach % 2:
        pieces = [earlier(own, reach, lambda source: source % 2 == 1)] + pieces
    return jnp.concatenate(pieces, axis=0), len(pieces) - 2


def attend_kernel(place, q_ref, kv_ref, start_ref, out_ref, q_all, top, total):
    rows = q_ref.shape[0]
    heads = q_ref.shape[1] // HEAD_SIZE
    for h in range(heads):
        q_all[h * rows : (h + 1) * rows, :] = q_ref[:, h * HEAD_SIZE : (h + 1) * HEAD_SIZE]
    top[...] = jnp.full_like(top, LOW)
    total[...] = jnp.zeros_like(total)
    q_low, first_start, last_start = place[1], place[2], place[3]
    factor = math.log2(math.e) / math.sqrt(HEAD_SIZE)

    def step(block, masked):
        low = pl.multiple_of(block * KEY_BLOCK, KEY_BLOCK)
        key = kv_ref[pl.ds(low, KEY_BLOCK), :HEAD_SIZE]
        value = kv_ref[pl.ds(low, KEY_BLOCK), HEAD_SIZE:]
        value = jnp.concatenate([value, jnp.ones_like(value)], axis=1)
        score = lax.dot_general(
            q_all[...], key, (((1,), (1,)), ((), ())), preferred_element_type=jnp.float32
        )
        score = score * factor
        if masked:
            key_pos = low + lax.broadcasted_iota(jnp.int32, (rows, KEY_BLOCK), 1)
            q_pos = q_low + lax.broadcasted_iota(jnp.int32, (rows, KEY_BLOCK), 0)
            seen = (key_pos >= start_ref[...]) & (key_pos <= q_pos)
            score = jnp.where(seen[None], score.reshape(heads, rows, KEY_BLOCK), LOW)
            score = score.reshape(heads * rows, KEY_BLOCK)
        old = top[...]
        new = jnp.maximum(old, jnp.max(score, axis=1, keepdims=True))
        weight = jnp.exp2(score - jnp.concatenate([new] * (KEY_BLOCK // HEAD_SIZE), axis=1))
        shrink = jnp.exp2(old - new)
        added = jnp.dot(weight.astype(jnp.bfloat16), value, preferred_element_type=jnp.float32)
        total[...] = total[...] * jnp.concatenate([shrink, shrink], axis=1) + added
        top[...] = new

    def loop(low, high, masked):
        def body(block, carry):
            step(block, masked)
            return carry

        lax.fori_loop(low, high, body, 0)

    begin = first_start // KEY_BLOCK
    end = (q_low + rows - 1) // KEY_BLOCK + 1
    inner_low = jnp.minimum((last_start + KEY_BLOCK - 1) // KEY_BLOCK, end)
    inner_high = jnp.maximum((q_low + 1) // KEY_BLOCK, inner_low)
    loop(begin, inner_low, True)
    loop(inner_low, inner_high, False)
    loop(inner_high, end, True)
    for h in range(heads):
        part = total[h * rows : (h + 1) * rows, :]
        out_ref[:, h * HEAD_SIZE : (h + 1) * HEAD_SIZE] = (
            part[:, :HEAD_SIZE] / part[:, HEAD_SIZE:]
        ).astype(out_ref.dtype)


def attend(block, queries, key_values, starts, own_low, rows):
    width = queries.shape[1]
    heads = width // HEAD_SIZE
    mine = lax.dynamic_slice_in_dim(starts, block * rows, rows, 0)
    place = jnp.stack([block, own_low + block * rows, mine[0], mine[rows - 1]]).astype(jnp.int32)
    pairs = heads * rows * key_values.shape[0] // 2
    return pl.pallas_call(
        attend_kernel,
        grid_spec=pltpu.PrefetchScalarGridSpec(
            num_scalar_prefetch=1,
            grid=(1,),
            in_specs=[
                pl.BlockSpec((rows, width), lambda i, place: (place[0], 0)),
                pl.BlockSpec(key_values.shape, lambda i, place: (0, 0)),
                pl.BlockSpec((rows, 1), lambda i, place: (place[0], 0)),
            ],
            out_specs=pl.BlockSpec((rows, width), lambda i, place: (0, 0)),
            scratch_shapes=[
                pltpu.VMEM((heads * rows, HEAD_SIZE), jnp.bfloat16),
                pltpu.VMEM((heads * rows, HEAD_SIZE), jnp.float32),
                pltpu.VMEM((heads * rows, 2 * HEAD_SIZE), jnp.float32),
            ],
        ),
        out_shape=jax.ShapeDtypeStruct((rows, width), jnp.bfloat16),
        compiler_params=pltpu.CompilerParams(vmem_limit_bytes=VMEM_BYTES),
        cost_estimate=pl.CostEstimate(
            flops=4 * pairs * HEAD_SIZE, bytes_accessed=4 * key_values.size, transcendentals=pairs
        ),
        name="attend",
    )(place, queries, key_values, starts[:, None])


def expert_kernel(own, by_x, by_y, far_a, far_b, pick, share, g0, u0, d0, g1, u1, d1,
                  out_own, out_x, out_y, out_a, out_b, taken, summed, given):
    step = pl.program_id(0)
    tiles = pl.num_programs(0) // 2
    slots = pick.shape[1] // 2
    half = far_a.shape[0]

    @pl.when(step == 0)
    def _():
        for b, block in enumerate((own, by_x, by_y, None)):
            if block is not None:
                rows = jnp.dot(pick[b], block[...], preferred_element_type=jnp.float32)
            else:
                rows = jnp.dot(pick[b, :, :half], far_a[...], preferred_element_type=jnp.float32)
                rows += jnp.dot(pick[b, :, half:], far_b[...], preferred_element_type=jnp.float32)
            rows = rows.astype(taken.dtype)
            for e in range(2):
                taken[e, b * slots : (b + 1) * slots, :] = rows[e * slots : (e + 1) * slots]

    def tile(e, gate_ref, up_ref, down_ref):
        rows = taken[e]
        gate = jnp.dot(rows, gate_ref[...], preferred_element_type=jnp.float32)
        up = jnp.dot(rows, up_ref[...], preferred_element_type=jnp.float32)
        hidden = (gate / (1.0 + jnp.exp(-gate)) * up).astype(jnp.bfloat16)
        part = jnp.dot(hidden, down_ref[...], preferred_element_type=jnp.float32)
        at = step - e * tiles

        @pl.when(at == 0)
        def _():
            summed[...] = part

        @pl.when(at > 0)
        def _():
            summed[...] += part

        @pl.when(at == tiles - 1)
        def _():
            given[e] = (summed[...] * share[e]).astype(given.dtype)

    @pl.when(step < tiles)
    def _():
        tile(0, g0, u0, d0)

    @pl.when(step >= tiles)
    def _():
        tile(1, g1, u1, d1)

    @pl.when(step == 2 * tiles - 1)
    def _():
        for b, block in enumerate((out_own, out_x, out_y, None)):
            rows = jnp.concatenate([given[e, b * slots : (b + 1) * slots, :] for e in range(2)])
            back = lax.dot_general(
                pick[b], rows, (((0,), (0,)), ((), ())), preferred_element_type=jnp.float32
            ).astype(jnp.bfloat16)
            if block is not None:
                block[...] = back
            else:
                out_a[...] = back[:half]
                out_b[...] = back[half:]


def run_experts(blocks, pick, share, own_weights, other_weights):
    rows, width = blocks[0].shape
    half = blocks[3].shape[0]
    ff = own_weights[0].shape[1]
    tile = math.gcd(ff, FF_TILE)
    tiles = ff // tile
    slots = share.shape[1]

    def whole(shape):
        return pl.BlockSpec(shape, lambda i: (0,) * len(shape))

    def first(i):
        return jnp.minimum(i, tiles - 1)

    def second(i):
        return jnp.maximum(i - tiles, 0)

    weights = []
    for at in (first, second):
        weights += [
            pl.BlockSpec((width, tile), lambda i, at=at: (0, at(i))),
            pl.BlockSpec((width, tile), lambda i, at=at: (0, at(i))),
            pl.BlockSpec((tile, width), lambda i, at=at: (at(i), 0)),
        ]
    shapes = [(rows, width)] * 3 + [(half, width), (rows - half, width)]
    return pl.pallas_call(
        expert_kernel,
        grid=(2 * tiles,),
        in_specs=[whole(s) for s in shapes] + [whole(pick.shape), whole(share.shape)] + weights,
        out_specs=[whole(s) for s in shapes],
        out_shape=[jax.ShapeDtypeStruct(s, jnp.bfloat16) for s in shapes],
        scratch_shapes=[
            pltpu.VMEM((2, slots, width), jnp.bfloat16),
            pltpu.VMEM((slots, width), jnp.float32),
            pltpu.VMEM((2, slots, width), jnp.bfloat16),
        ],
        compiler_params=pltpu.CompilerParams(vmem_limit_bytes=VMEM_BYTES),
        cost_estimate=pl.CostEstimate(
            flops=12 * slots * width * ff,
            bytes_accessed=12 * width * ff + 16 * rows * width,
            transcendentals=2 * slots * ff,
        ),
        name="experts",
    )(*blocks, pick, share, *own_weights, *other_weights)


def spread(block):
    half = block.shape[0] // 2
    by_x, by_y = swap_x(block), swap_y(block)
    return block, by_x, by_y, swap_y(by_x[:half]), swap_x(by_y[half:])


def collect(own, by_x, by_y, far_a, far_b):
    half = far_a.shape[0]
    from_a, from_b = swap_x(far_a), swap_y(far_b)
    by_y = jnp.concatenate([by_y[:half] + from_a, by_y[half:]])
    by_x = jnp.concatenate([by_x[:half], by_x[half:] + from_b])
    return own.astype(jnp.float32) + swap_x(by_x).astype(jnp.float32) + swap_y(by_y).astype(jnp.float32)


def routing(ids, gates, expert_count, slots):
    dev_size = lax.axis_size("dev")
    planes = dev_size // 2
    dense = jnp.sum(
        jnp.where(
            ids.T[None] == jnp.arange(expert_count, dtype=jnp.int32)[:, None, None], gates.T[None], 0.0
        ),
        axis=1,
    )
    pair = jnp.stack([dense, swap_x(dense)])
    four = jnp.concatenate([pair, swap_y(pair)])
    every = jnp.stack([four] + [turn(four, k) for k in range(1, planes)])
    me = lax.axis_index("grp") * dev_size + lax.axis_index("dev")
    mine = jnp.stack(
        [lax.dynamic_index_in_dim(every, e, 2, keepdims=False) for e in (me, me ^ 1)], axis=2
    )
    named = mine > 0
    tokens = mine.shape[-1]
    before = jnp.triu(jnp.ones((tokens, tokens), jnp.bfloat16), 1)
    rank = jnp.dot(named.astype(jnp.bfloat16), before, preferred_element_type=jnp.float32)
    slot = jnp.arange(slots, dtype=jnp.int32).astype(jnp.float32)
    chosen = named[..., None, :] & (rank[..., None, :] == slot[:, None])
    share = jnp.sum(jnp.where(chosen, mine[..., None, :], 0.0), axis=-1)
    pick = chosen.astype(jnp.bfloat16).reshape(planes, 4, 2 * slots, tokens)
    share = share.transpose(0, 2, 1, 3).reshape(planes, 2, 4 * slots, 1)
    return pick, share


def shards(
    queries,
    keys,
    values,
    doc_ids,
    out_weight,
    norm_gain,
    expert_ids,
    gate_values,
    expert_gate,
    expert_up,
    expert_down,
):
    own_rows = queries.shape[0]
    grp_size = lax.axis_size("grp")
    dev_size = lax.axis_size("dev")
    planes = dev_size // 2
    group, device = lax.axis_index("grp"), lax.axis_index("dev")
    dev_rows = own_rows // grp_size
    width = out_weight.shape[1]
    top_count = expert_ids.shape[2]
    expert_count = grp_size * dev_size
    capacity = max(2, 3 * dev_rows * top_count // (2 * expert_count))
    slots = -(-capacity // 16) * 16
    doc_reach = dev_size * own_rows // 2 + own_rows
    reach = min(dev_size - 1, (doc_reach + own_rows - 1) // own_rows)

    key_values, ahead = gather_keys(keys, values, reach)
    own_low = (ahead + device % 2) * own_rows
    own_docs = lax.dynamic_slice_in_dim(doc_ids, device * own_rows, own_rows, 0)
    starts = jnp.sum((doc_ids[None, :] < own_docs[:, None]).astype(jnp.int32), axis=1)
    starts = starts - device * own_rows + own_low

    pick, share = routing(expert_ids[0], gate_values[0], expert_count, slots)
    own_weights = [expert_gate[0], expert_up[0], expert_down[0]]

    def part(block):
        attended = attend(block, queries, key_values, starts, own_low, dev_rows)
        return jnp.dot(attended, out_weight, preferred_element_type=jnp.float32)

    half = dev_rows // 2
    far = part(group ^ 3).astype(jnp.bfloat16)
    by_x = part(group ^ 1).astype(jnp.bfloat16)
    by_y = part(group ^ 2).astype(jnp.bfloat16)
    own = part(group)
    projected = collect(own, by_x, by_y, far[:half], far[half:])
    other_weights = [swap_core(after(w, far)) for w in own_weights]
    normed = (
        projected
        * lax.rsqrt(jnp.mean(projected * projected, axis=-1, keepdims=True) + 1e-06)
        * norm_gain
    ).astype(jnp.bfloat16)

    order = sorted(range(1, planes), key=lambda k: min(k, planes - k))
    turned, last = {0: normed}, normed
    for k in order:
        last = turned[k] = turn(after(normed, last), k)
    results = {}
    for k in [0] + order:
        results[k] = run_experts(spread(turned[k]), pick[k], share[k], own_weights, other_weights)
    mixed = 0.0
    for k in list(range(1, planes)) + [0]:
        summed = collect(*results[k])
        if k:
            summed = turn(summed.astype(jnp.bfloat16), planes - k).astype(jnp.float32)
        mixed = mixed + summed
    return (projected + mixed).astype(jnp.bfloat16)[None]


def solution(mesh):
    return jax.shard_map(
        shards,
        mesh=mesh,
        in_specs=(
            P("dev", "grp"),
            P("dev", "grp"),
            P("dev", "grp"),
            P(),
            P("grp", None),
            P(),
            P("dev", "grp", None),
            P("dev", "grp", None),
            P(("grp", "dev"), None, None),
            P(("grp", "dev"), None, None),
            P(("grp", "dev"), None, None),
        ),
        out_specs=P("dev", "grp", None),
        check_vma=False,
    )
```

```python
import functools
import math

import jax
import jax.numpy as jnp
from jax import lax
from jax.experimental import pallas as pl
from jax.experimental.pallas import tpu as pltpu
from jax.sharding import PartitionSpec as P

HEAD_SIZE = 128
KEY_BLOCK = 512
SPLIT = 8
FF_TILE = 256
VMEM_BYTES = 56 * 1024 * 1024
LOW = -1e30


def after(value, *others):
    return lax.optimization_barrier((value, *others))[0]


def swap_x(value):
    return lax.ppermute(value, "grp", [(i, i ^ 1) for i in range(lax.axis_size("grp"))])


def swap_y(value):
    return lax.ppermute(value, "grp", [(i, i ^ 2) for i in range(lax.axis_size("grp"))])


def swap_core(value):
    return lax.ppermute(value, "dev", [(i, i ^ 1) for i in range(lax.axis_size("dev"))])


def turn(value, planes):
    count = lax.axis_size("dev")
    return lax.ppermute(value, "dev", [(i, (i - 2 * planes) % count) for i in range(count)])


def earlier(value, steps, sources=lambda source: True):
    count = lax.axis_size("dev")
    pairs = [(i, i + steps) for i in range(count - steps) if sources(i)]
    return lax.ppermute(value, "dev", pairs)


def hold_kernel(*refs):
    del refs


def hold(values, *waits):
    anywhere = pl.BlockSpec(memory_space=pl.ANY)
    return pl.pallas_call(
        hold_kernel,
        in_specs=[anywhere] * (len(values) + len(waits)),
        out_specs=[anywhere] * len(values),
        out_shape=[jax.ShapeDtypeStruct(v.shape, v.dtype) for v in values],
        input_output_aliases={i: i for i in range(len(values))},
        cost_estimate=pl.CostEstimate(flops=0, bytes_accessed=0, transcendentals=0),
        name="hold",
    )(*values, *waits)


def gather_keys(keys, values, reach):
    own = jnp.concatenate([keys, values], axis=1)
    whole = reach // 2
    lanes = [own] + [earlier(own, 2 * j) for j in range(1, whole + 1)]
    pieces = [piece for lane in lanes[::-1] for piece in (lane, swap_core(lane))]
    if reach % 2:
        pieces = [earlier(own, reach, lambda source: source % 2 == 1)] + pieces
    return pieces


def attend_kernel(place, bounds, *refs, shards, waits):
    q_ref, start_ref = refs[:2]
    pieces = refs[2 : 2 + shards]
    out_ref, q_all, kv_ref, top, total = refs[2 + shards + waits :]
    size = pieces[0].shape[0]
    core = place[1]
    for i, piece in enumerate(pieces):
        lone = shards % 2
        if i < lone:
            at = 0
        else:
            pair = i - (i - lone) % 2
            at = pair + (core if pair == i else 1 - core)
        kv_ref[pl.ds(pl.multiple_of(at * size, size), size), :] = piece[...]
    rows = q_ref.shape[0]
    heads = q_ref.shape[1] // HEAD_SIZE
    for h in range(heads):
        q_all[h * rows : (h + 1) * rows, :] = q_ref[:, h * HEAD_SIZE : (h + 1) * HEAD_SIZE]
    top[...] = jnp.full_like(top, LOW)
    total[...] = jnp.zeros_like(total)
    block_index = place[0]
    q_low = bounds[0] + block_index * rows
    first_start, last_start = bounds[1 + 2 * block_index], bounds[2 + 2 * block_index]
    factor = math.log2(math.e) / math.sqrt(HEAD_SIZE)

    def step(block, masked):
        low = pl.multiple_of(block * KEY_BLOCK, KEY_BLOCK)
        key = kv_ref[pl.ds(low, KEY_BLOCK), :HEAD_SIZE]
        value = kv_ref[pl.ds(low, KEY_BLOCK), HEAD_SIZE:]
        value = jnp.concatenate([value, jnp.ones_like(value)], axis=1)
        if masked:
            key_pos = low + lax.broadcasted_iota(jnp.int32, (rows, KEY_BLOCK), 1)
            q_pos = q_low + lax.broadcasted_iota(jnp.int32, (rows, KEY_BLOCK), 0)
            seen = (key_pos >= start_ref[...]) & (key_pos <= q_pos)
        part_heads = heads // SPLIT
        size = part_heads * rows
        scores = []
        for r in range(SPLIT):
            scores.append(lax.dot_general(
                q_all[r * size : (r + 1) * size, :], key, (((1,), (1,)), ((), ())), preferred_element_type=jnp.float32
            ))
        for r in range(SPLIT):
            span = slice(r * size, (r + 1) * size)
            score = scores[r] * factor
            if masked:
                score = jnp.where(seen[None], score.reshape(part_heads, rows, KEY_BLOCK), LOW)
                score = score.reshape(size, KEY_BLOCK)
            old = top[span, :]
            new = jnp.maximum(old, jnp.max(score, axis=1, keepdims=True))
            weight = jnp.exp2(score - jnp.concatenate([new] * (KEY_BLOCK // HEAD_SIZE), axis=1))
            shrink = jnp.exp2(old - new)
            added = jnp.dot(weight.astype(jnp.bfloat16), value, preferred_element_type=jnp.float32)
            total[span, :] = total[span, :] * jnp.concatenate([shrink, shrink], axis=1) + added
            top[span, :] = new

    def loop(low, high, masked):
        def body(block, carry):
            step(block, masked)
            return carry

        lax.fori_loop(low, high, body, 0)

    begin = first_start // KEY_BLOCK
    end = (q_low + rows - 1) // KEY_BLOCK + 1
    inner_low = jnp.minimum((last_start + KEY_BLOCK - 1) // KEY_BLOCK, end)
    inner_high = jnp.maximum((q_low + 1) // KEY_BLOCK, inner_low)
    loop(begin, inner_low, True)
    loop(inner_low, inner_high, False)
    loop(inner_high, end, True)
    for h in range(heads):
        part = total[h * rows : (h + 1) * rows, :]
        out_ref[:, h * HEAD_SIZE : (h + 1) * HEAD_SIZE] = (
            part[:, :HEAD_SIZE] / part[:, HEAD_SIZE:]
        ).astype(out_ref.dtype)


def attend(block, queries, pieces, starts, bounds, rows, waits=()):
    width = queries.shape[1]
    heads = width // HEAD_SIZE
    length = len(pieces) * pieces[0].shape[0]
    pairs = heads * rows * length // 2
    place = jnp.stack([block, lax.axis_index("dev") % 2]).astype(jnp.int32)
    return pl.pallas_call(
        functools.partial(attend_kernel, shards=len(pieces), waits=len(waits)),
        grid_spec=pltpu.PrefetchScalarGridSpec(
            num_scalar_prefetch=2,
            grid=(1,),
            in_specs=[
                pl.BlockSpec((rows, width), lambda i, place, bounds: (place[0], 0)),
                pl.BlockSpec((rows, 1), lambda i, place, bounds: (place[0], 0)),
            ]
            + [pl.BlockSpec(p.shape, lambda i, place, bounds: (0, 0)) for p in pieces]
            + [pl.BlockSpec(memory_space=pl.ANY)] * len(waits),
            out_specs=pl.BlockSpec((rows, width), lambda i, place, bounds: (0, 0)),
            scratch_shapes=[
                pltpu.VMEM((heads * rows, HEAD_SIZE), jnp.bfloat16),
                pltpu.VMEM((length, 2 * HEAD_SIZE), jnp.bfloat16),
                pltpu.VMEM((heads * rows, HEAD_SIZE), jnp.float32),
                pltpu.VMEM((heads * rows, 2 * HEAD_SIZE), jnp.float32),
            ],
        ),
        out_shape=jax.ShapeDtypeStruct((rows, width), jnp.bfloat16),
        compiler_params=pltpu.CompilerParams(vmem_limit_bytes=VMEM_BYTES),
        cost_estimate=pl.CostEstimate(
            flops=4 * pairs * HEAD_SIZE, bytes_accessed=4 * length * HEAD_SIZE, transcendentals=pairs
        ),
        name="attend",
    )(place, bounds, queries, starts[:, None], *pieces, *waits)


def feed_kernel(*refs, blocks, first, waits):
    step = pl.program_id(0)
    last = pl.num_programs(0) - 1
    refs = list(refs)
    incoming = [refs.pop(0) for _ in range(5 * blocks)] if first else None
    slot_of, gates, gate_ref, up_ref, down_ref = (refs.pop(0) for _ in range(5))
    if not first:
        taken, earlier_given = refs.pop(0), refs.pop(0)
    refs = refs[waits:]
    if first:
        given, other, taken, summed = refs
    else:
        outgoing, (given, summed) = refs[: 5 * blocks], refs[5 * blocks :]
    tokens = slot_of.shape[3]
    half = tokens // 2
    slots = given.shape[0] // (2 * blocks)
    each = slots // 2

    def chosen(p, e, b):
        at = 2 * p + b
        mine = slot_of[at // 4, e, at % 4 : at % 4 + 1, :]
        return lax.broadcasted_iota(jnp.int32, (each, tokens), 0) == mine

    def pick(p):
        lines = []
        for e in range(2):
            for b in range(2):
                found = chosen(p, e, b).astype(jnp.float32)
                zeros = jnp.zeros_like(found)
                lines.append(jnp.concatenate([zeros, found] if b else [found, zeros], axis=1))
        return jnp.concatenate(lines).astype(jnp.bfloat16)

    def share(e):
        parts = []
        for p in range(2 * blocks):
            for b in range(2):
                at = 2 * p + b
                gate = gates[at // 4, e, at % 4 : at % 4 + 1, :]
                parts.append(jnp.sum(jnp.where(chosen(p, e, b), gate, 0.0), axis=1, keepdims=True))
        return jnp.concatenate(parts)

    if first:

        @pl.when(step == 0)
        def _():
            for p in range(2 * blocks):
                at = 5 * (p // 2) + 2 * (p % 2)
                pieces = incoming[at : at + 2 + p % 2]
                held = jnp.concatenate([piece[...] for piece in pieces])
                found = jnp.dot(pick(p), held, preferred_element_type=jnp.float32)
                found = found.astype(taken.dtype)
                taken[p * slots : (p + 1) * slots, :] = found[:slots]
                other[p * slots : (p + 1) * slots, :] = found[slots:]

    rows = taken[...]
    gate = jnp.dot(rows, gate_ref[...], preferred_element_type=jnp.float32)
    up = jnp.dot(rows, up_ref[...], preferred_element_type=jnp.float32)
    hidden = (gate / (1.0 + jnp.exp(-gate)) * up).astype(jnp.bfloat16)
    part = jnp.dot(hidden, down_ref[...], preferred_element_type=jnp.float32)

    @pl.when(step == 0)
    def _():
        summed[...] = part

    @pl.when(step > 0)
    def _():
        summed[...] += part

    @pl.when(step == last)
    def _():
        given[...] = (summed[...] * share(0 if first else 1)).astype(given.dtype)
        if first:
            return
        for p in range(2 * blocks):
            at = 5 * (p // 2) + 2 * (p % 2)
            place = slice(p * slots, (p + 1) * slots)
            rows = jnp.concatenate([earlier_given[place, :], given[place, :]])
            back = lax.dot_general(
                pick(p), rows, (((0,), (0,)), ((), ())), preferred_element_type=jnp.float32
            ).astype(jnp.bfloat16)
            outgoing[at][...] = back[:tokens]
            if p % 2 == 0:
                outgoing[at + 1][...] = back[tokens:]
            else:
                outgoing[at + 1][...] = back[tokens : tokens + half]
                outgoing[at + 2][...] = back[tokens + half :]


def feed(first, inputs, slot_of, gates, slots, weights, extra, rows, waits=()):
    width, ff = weights[0].shape
    tile = math.gcd(ff, FF_TILE)
    blocks = slot_of.shape[0]
    slots = 4 * blocks * slots

    def whole(shape):
        return pl.BlockSpec(shape, lambda i: (0,) * len(shape))

    shapes = ([(rows, width)] * 3 + [(rows // 2, width), (rows - rows // 2, width)]) * blocks
    operands = [*inputs, slot_of, gates, *weights, *extra]
    specs = [whole(v.shape) for v in operands]
    at = len(inputs) + 2
    specs[at : at + 3] = [
        pl.BlockSpec((width, tile), lambda i: (0, i)),
        pl.BlockSpec((width, tile), lambda i: (0, i)),
        pl.BlockSpec((tile, width), lambda i: (i, 0)),
    ]
    specs += [pl.BlockSpec(memory_space=pl.ANY)] * len(waits)
    results = [(slots, width)] * 2 if first else shapes
    kept = pltpu.VMEM((slots, width), jnp.bfloat16)
    return pl.pallas_call(
        functools.partial(feed_kernel, blocks=blocks, first=first, waits=len(waits)),
        grid=(ff // tile,),
        in_specs=specs,
        out_specs=[whole(s) for s in results],
        out_shape=[jax.ShapeDtypeStruct(s, jnp.bfloat16) for s in results],
        scratch_shapes=[kept, pltpu.VMEM((slots, width), jnp.float32)],
        compiler_params=pltpu.CompilerParams(vmem_limit_bytes=VMEM_BYTES),
        cost_estimate=pl.CostEstimate(
            flops=6 * slots * width * ff,
            bytes_accessed=6 * width * ff + 12 * blocks * rows * width,
            transcendentals=slots * ff,
        ),
        name="feed_first" if first else "feed_second",
    )(*operands, *waits)


def collect_near(own, by_x, by_y, from_a, from_b, *waits):
    half = from_a.shape[0]
    if waits:
        by_x, by_y = hold([by_x, by_y], *waits)
    by_y = jnp.concatenate([by_y[:half] + from_a, by_y[half:]])
    by_x = jnp.concatenate([by_x[:half], by_x[half:] + from_b])
    return own, swap_x(by_x), swap_y(by_y)


def add_up(parts):
    return sum(part.astype(jnp.float32) for part in parts)


def routing(ids, gates, expert_count, waits):
    dev_size = lax.axis_size("dev")
    planes = dev_size // 2
    named = ids.T[None] == jnp.arange(expert_count, dtype=jnp.int32)[:, None, None]
    [dense] = hold([jnp.sum(jnp.where(named, gates.T[None], 0.0), axis=1)], *waits)
    pair = jnp.stack([dense, swap_x(dense)])
    four = jnp.concatenate([pair, swap_y(pair)])
    every = jnp.stack([four] + [turn(four, k) for k in range(1, planes)])
    me = lax.axis_index("grp") * dev_size + lax.axis_index("dev")
    mine = jnp.stack(
        [lax.dynamic_index_in_dim(every, e, 2, keepdims=False) for e in (me, me ^ 1)], axis=1
    )
    named = mine > 0
    tokens = mine.shape[-1]
    before = jnp.triu(jnp.ones((tokens, tokens), jnp.bfloat16), 1)
    rank = jnp.dot(named.astype(jnp.bfloat16), before, preferred_element_type=jnp.float32)
    return jnp.where(named, rank, -1.0).astype(jnp.int32), mine, (pair, four)


def shards(
    queries,
    keys,
    values,
    doc_ids,
    out_weight,
    norm_gain,
    expert_ids,
    gate_values,
    expert_gate,
    expert_up,
    expert_down,
):
    own_rows = queries.shape[0]
    grp_size = lax.axis_size("grp")
    dev_size = lax.axis_size("dev")
    planes = dev_size // 2
    group, device = lax.axis_index("grp"), lax.axis_index("dev")
    dev_rows = own_rows // grp_size
    width = out_weight.shape[1]
    top_count = expert_ids.shape[2]
    expert_count = grp_size * dev_size
    capacity = max(2, 3 * dev_rows * top_count // (2 * expert_count))
    slots = -(-capacity // 16) * 16
    doc_reach = dev_size * own_rows // 2 + own_rows
    reach = min(dev_size - 1, (doc_reach + own_rows - 1) // own_rows)

    pieces = gather_keys(keys, values, reach)
    own_low = (len(pieces) - 2 + device % 2) * own_rows
    own_docs = lax.dynamic_slice_in_dim(doc_ids, device * own_rows, own_rows, 0)
    starts = jnp.sum((doc_ids[None, :] < own_docs[:, None]).astype(jnp.int32), axis=1)
    starts = starts - device * own_rows + own_low
    ends = jnp.stack([starts[::dev_rows], starts[dev_rows - 1 :: dev_rows]], axis=1)
    bounds = jnp.concatenate([own_low[None], ends.reshape(-1)]).astype(jnp.int32)

    slot_of, gates, steps = routing(expert_ids[0], gate_values[0], expert_count, pieces[-2:])
    own_weights = [expert_gate[0], expert_up[0], expert_down[0]]
    other_weights = [swap_core(w) for w in own_weights]

    def part(block, *waits):
        attended = attend(block, queries, pieces, starts, bounds, dev_rows, waits)
        return jnp.dot(attended, out_weight, preferred_element_type=jnp.float32)

    half = dev_rows // 2
    far = part(group ^ 3).astype(jnp.bfloat16)
    from_a, from_b = swap_x(far[:half]), swap_y(far[half:])
    by_x = part(group ^ 1, far, steps[0], *other_weights).astype(jnp.bfloat16)
    by_y = part(group ^ 2, by_x, steps[1]).astype(jnp.bfloat16)
    own = part(group, slot_of, gates, from_a, from_b)
    projected = add_up(collect_near(own, by_x, by_y, from_a, from_b))
    normed = (
        projected
        * lax.rsqrt(jnp.mean(projected * projected, axis=-1, keepdims=True) + 1e-06)
        * norm_gain
    ).astype(jnp.bfloat16)

    order = list(range(planes))
    turned = order[1:] + order[:1]
    sets = [turned[i : i + 2] for i in range(0, planes, 2)]
    blocks, done = {}, {}

    def feed_first(members, *waits):
        routes = [jnp.stack([part[k] for k in members]) for part in (slot_of, gates)]
        inputs = [b for k in members for b in blocks[k]]
        results = feed(True, inputs, *routes, slots, own_weights, [], dev_rows, waits)
        return members, routes, *results

    def feed_second(state, *waits):
        members, routes, given, other = state
        out = feed(False, [], *routes, slots, other_weights, [other, given], dev_rows, waits)
        for i, k in enumerate(members):
            done[k] = out[5 * i : 5 * i + 5]
        return out[0]

    def relay(near, *waits):
        first, second = halves(*near, *waits) if waits else (near[0][:half], near[1][half:])
        return swap_y(first), swap_x(second)

    near, sent, fars = (), [], [(), ()]

    def launch(k):
        nonlocal near
        block = normed
        if k:
            block = jnp.copy(normed)
            if len(sent) > 1:
                [block] = hold([block], *sent[-2])
            [block] = hold([turn(block, k)], *near, *fars[-2])
        near = swap_x(block), swap_y(block)
        blocks[k] = [block]

    def relay(k, *waits):
        nonlocal near
        near = hold(near, *waits) if waits else near
        sent.append((near[0][:half], near[1][half:]))
        far = swap_y(sent[-1][0]), swap_x(sent[-1][1])
        fars.append(far)
        blocks[k] += [*near, *far]
        return far

    launch(0)
    far = relay(0)
    for i, members in enumerate(sets[:-1]):
        for k in members:
            if k not in blocks:
                launch(k)
                relay(k)
        following = next(k for k in sets[i + 1] if k)
        state = feed_first(members)
        launch(following)
        far = relay(following, state[2])
        feed_second(state, *near)

    early = [k for members in sets[:-1][::-1] for k in members[::-1]]
    late = [k for k in sets[-1] if k] + [0]
    froms, sums = {}, []

    def far_part(k):
        froms[k] = swap_x(done[k][3]), swap_y(done[k][4])
        return froms[k]

    def near_part(k, *waits):
        parts = collect_near(*done[k][:3], *froms[k], *waits)
        summed = add_up(parts)
        if k:
            summed = turn(summed.astype(jnp.bfloat16), planes - k).astype(jnp.float32)
        sums.append(summed)
        return parts[1:]

    def held(k, *waits):
        done[k] = [*done[k][:3], *hold(done[k][3:5], *waits)]

    chain = far
    for k in early[:1]:
        held(k, *chain)
        chain = far_part(k)
    state = feed_first(sets[-1], *chain)
    arrived = ()
    for k in early[:1]:
        arrived = near_part(k)
    for k in early[1:]:
        held(k, *chain)
        chain = far_part(k)
    feed_second(state, *arrived, *chain)
    for k in early[1:]:
        arrived = near_part(k, state[2])
    chain = arrived
    for k in late:
        held(k, *chain)
        chain = far_part(k)
        near_part(k)
    return (projected + sum(sums)).astype(jnp.bfloat16)[None]


def solution(mesh):
    return jax.shard_map(
        shards,
        mesh=mesh,
        in_specs=(
            P("dev", "grp"),
            P("dev", "grp"),
            P("dev", "grp"),
            P(),
            P("grp", None),
            P(),
            P("dev", "grp", None),
            P("dev", "grp", None),
            P(("grp", "dev"), None, None),
            P(("grp", "dev"), None, None),
            P(("grp", "dev"), None, None),
        ),
        out_specs=P("dev", "grp", None),
        check_vma=False,
    )
```

```python
import functools
import math

import jax
import jax.numpy as jnp
from jax import lax
from jax.experimental import pallas as pl
from jax.experimental.pallas import tpu as pltpu
from jax.sharding import PartitionSpec as P

HEAD_SIZE = 128
KEY_BLOCK = 512
SPLIT = 8
OUT_TILE = 512
VMEM_BYTES = 56 * 1024 * 1024
LOW = -1e30


def after(value, *others):
    return lax.optimization_barrier((value, *others))[0]


def swap_x(value):
    return lax.ppermute(value, "grp", [(i, i ^ 1) for i in range(lax.axis_size("grp"))])


def swap_y(value):
    return lax.ppermute(value, "grp", [(i, i ^ 2) for i in range(lax.axis_size("grp"))])


def swap_core(value):
    return lax.ppermute(value, "dev", [(i, i ^ 1) for i in range(lax.axis_size("dev"))])


def turn(value, planes):
    count = lax.axis_size("dev")
    return lax.ppermute(value, "dev", [(i, (i - 2 * planes) % count) for i in range(count)])


def earlier(value, steps, sources=lambda source: True):
    count = lax.axis_size("dev")
    pairs = [(i, i + steps) for i in range(count - steps) if sources(i)]
    return lax.ppermute(value, "dev", pairs)


def hold_kernel(*refs):
    del refs


def hold(values, *waits):
    anywhere = pl.BlockSpec(memory_space=pl.ANY)
    return pl.pallas_call(
        hold_kernel,
        in_specs=[anywhere] * (len(values) + len(waits)),
        out_specs=[anywhere] * len(values),
        out_shape=[jax.ShapeDtypeStruct(v.shape, v.dtype) for v in values],
        input_output_aliases={i: i for i in range(len(values))},
        cost_estimate=pl.CostEstimate(flops=0, bytes_accessed=0, transcendentals=0),
        name="hold",
    )(*values, *waits)


def gather_keys(keys, values, reach):
    own = jnp.concatenate([keys, values], axis=1)
    whole = reach // 2
    lanes = [own]
    for _ in range(whole):
        lanes.append(earlier(lanes[-1], 2))
    pieces = [piece for lane in lanes[::-1] for piece in (lane, swap_core(lane))]
    if reach % 2:
        pieces = [earlier(lanes[-1], 1, lambda source: source % 2 == 1)] + pieces
    return pieces


def attend_kernel(bounds, *refs, shards, waits, mask):
    q_ref, start_ref = refs[:2]
    pieces = refs[2 : 2 + shards]
    out_ref, q_all, kv_ref, top, total = refs[2 + shards + waits :]
    size = pieces[0].shape[0]
    core = bounds[2]
    for i, piece in enumerate(pieces):
        lone = shards % 2
        if i < lone:
            at = 0
        else:
            pair = i - (i - lone) % 2
            at = pair + (core if pair == i else 1 - core)
        kv_ref[pl.ds(pl.multiple_of(at * size, size), size), :] = piece[...]
    rows = q_ref.shape[0]
    heads = q_ref.shape[1] // HEAD_SIZE
    for h in range(heads):
        q_all[h * rows : (h + 1) * rows, :] = q_ref[:, h * HEAD_SIZE : (h + 1) * HEAD_SIZE]
    top[...] = jnp.full_like(top, LOW)
    total[...] = jnp.zeros_like(total)
    block_index = bounds[1] ^ mask
    q_low = bounds[0] + block_index * rows
    first_start, last_start = bounds[3 + 2 * block_index], bounds[4 + 2 * block_index]
    factor = math.log2(math.e) / math.sqrt(HEAD_SIZE)

    def step(block, masked):
        low = pl.multiple_of(block * KEY_BLOCK, KEY_BLOCK)
        key = kv_ref[pl.ds(low, KEY_BLOCK), :HEAD_SIZE]
        value = kv_ref[pl.ds(low, KEY_BLOCK), HEAD_SIZE:]
        value = jnp.concatenate([value, jnp.ones_like(value)], axis=1)
        if masked:
            key_pos = low + lax.broadcasted_iota(jnp.int32, (rows, KEY_BLOCK), 1)
            q_pos = q_low + lax.broadcasted_iota(jnp.int32, (rows, KEY_BLOCK), 0)
            seen = (key_pos >= start_ref[...]) & (key_pos <= q_pos)
        part_heads = heads // SPLIT
        size = part_heads * rows
        scores = []
        for r in range(SPLIT):
            scores.append(lax.dot_general(
                q_all[r * size : (r + 1) * size, :], key, (((1,), (1,)), ((), ())), preferred_element_type=jnp.float32
            ))
        for r in range(SPLIT):
            span = slice(r * size, (r + 1) * size)
            score = scores[r] * factor
            if masked:
                score = jnp.where(seen[None], score.reshape(part_heads, rows, KEY_BLOCK), LOW)
                score = score.reshape(size, KEY_BLOCK)
            old = top[span, :]
            new = jnp.maximum(old, jnp.max(score, axis=1, keepdims=True))
            weight = jnp.exp2(score - jnp.concatenate([new] * (KEY_BLOCK // HEAD_SIZE), axis=1))
            shrink = jnp.exp2(old - new)
            added = jnp.dot(weight.astype(jnp.bfloat16), value, preferred_element_type=jnp.float32)
            total[span, :] = total[span, :] * jnp.concatenate([shrink, shrink], axis=1) + added
            top[span, :] = new

    def loop(low, high, masked):
        def body(block, carry):
            step(block, masked)
            return carry

        lax.fori_loop(low, high, body, 0)

    begin = first_start // KEY_BLOCK
    end = (q_low + rows - 1) // KEY_BLOCK + 1
    inner_low = jnp.minimum((last_start + KEY_BLOCK - 1) // KEY_BLOCK, end)
    inner_high = jnp.maximum((q_low + 1) // KEY_BLOCK, inner_low)
    loop(begin, inner_low, True)
    loop(inner_low, inner_high, False)
    loop(inner_high, end, True)
    for h in range(heads):
        part = total[h * rows : (h + 1) * rows, :]
        out_ref[:, h * HEAD_SIZE : (h + 1) * HEAD_SIZE] = (
            part[:, :HEAD_SIZE] / part[:, HEAD_SIZE:]
        ).astype(out_ref.dtype)


def attend(mask, queries, pieces, starts, bounds, rows, waits=()):
    width = queries.shape[1]
    heads = width // HEAD_SIZE
    length = len(pieces) * pieces[0].shape[0]
    pairs = heads * rows * length // 2
    return pl.pallas_call(
        functools.partial(attend_kernel, shards=len(pieces), waits=len(waits), mask=mask),
        grid_spec=pltpu.PrefetchScalarGridSpec(
            num_scalar_prefetch=1,
            grid=(1,),
            in_specs=[
                pl.BlockSpec((rows, width), lambda i, bounds: (bounds[1] ^ mask, 0)),
                pl.BlockSpec((rows, 1), lambda i, bounds: (bounds[1] ^ mask, 0)),
            ]
            + [pl.BlockSpec(p.shape, lambda i, bounds: (0, 0)) for p in pieces]
            + [pl.BlockSpec(memory_space=pl.ANY)] * len(waits),
            out_specs=pl.BlockSpec((rows, width), lambda i, bounds: (0, 0)),
            scratch_shapes=[
                pltpu.VMEM((heads * rows, HEAD_SIZE), jnp.bfloat16),
                pltpu.VMEM((length, 2 * HEAD_SIZE), jnp.bfloat16),
                pltpu.VMEM((heads * rows, HEAD_SIZE), jnp.float32),
                pltpu.VMEM((heads * rows, 2 * HEAD_SIZE), jnp.float32),
            ],
        ),
        out_shape=jax.ShapeDtypeStruct((rows, width), jnp.bfloat16),
        compiler_params=pltpu.CompilerParams(vmem_limit_bytes=VMEM_BYTES),
        cost_estimate=pl.CostEstimate(
            flops=4 * pairs * HEAD_SIZE, bytes_accessed=4 * length * HEAD_SIZE, transcendentals=pairs
        ),
        name="attend",
    )(bounds, queries, starts[:, None], *pieces, *waits)


def feed_kernel(*refs, blocks, first, waits):
    refs = list(refs)
    gate_buf, up_buf, down_buf, sems = refs[-4:]
    del refs[-4:]
    incoming = [refs.pop(0) for _ in range(5 * blocks)] if first else None
    slot_of, gates, gate_ref, up_ref, down_ref = (refs.pop(0) for _ in range(5))
    if not first:
        taken, earlier_given = refs.pop(0), refs.pop(0)
    refs = refs[waits:]
    if first:
        given, other, taken = refs
    else:
        outgoing, given = refs[: 5 * blocks], refs[5 * blocks]
    loads = [
        pltpu.make_async_copy(source, target, sems.at[i])
        for i, (source, target) in enumerate(
            ((gate_ref, gate_buf), (up_ref, up_buf), (down_ref, down_buf))
        )
    ]
    for load in loads:
        load.start()
    tokens = slot_of.shape[3]
    half = tokens // 2
    slots = given.shape[0] // (2 * blocks)
    each = slots // 2

    def chosen(p, e, b):
        at = 2 * p + b
        mine = slot_of[at // 4, e, at % 4 : at % 4 + 1, :]
        return lax.broadcasted_iota(jnp.int32, (each, tokens), 0) == mine

    def pick(p):
        lines = []
        for e in range(2):
            for b in range(2):
                found = chosen(p, e, b).astype(jnp.float32)
                zeros = jnp.zeros_like(found)
                lines.append(jnp.concatenate([zeros, found] if b else [found, zeros], axis=1))
        return jnp.concatenate(lines).astype(jnp.bfloat16)

    def share(e):
        parts = []
        for p in range(2 * blocks):
            for b in range(2):
                at = 2 * p + b
                gate = gates[at // 4, e, at % 4 : at % 4 + 1, :]
                parts.append(jnp.sum(jnp.where(chosen(p, e, b), gate, 0.0), axis=1, keepdims=True))
        return jnp.concatenate(parts)

    if first:
        for p in range(2 * blocks):
            at = 5 * (p // 2) + 2 * (p % 2)
            held = jnp.concatenate([piece[...] for piece in incoming[at : at + 2 + p % 2]])
            found = jnp.dot(pick(p), held, preferred_element_type=jnp.float32).astype(taken.dtype)
            taken[p * slots : (p + 1) * slots, :] = found[:slots]
            other[p * slots : (p + 1) * slots, :] = found[slots:]

    rows = taken[...]
    loads[0].wait()
    gate = jnp.dot(rows, gate_buf[...], preferred_element_type=jnp.float32)
    loads[1].wait()
    up = jnp.dot(rows, up_buf[...], preferred_element_type=jnp.float32)
    hidden = (gate / (1.0 + jnp.exp(-gate)) * up).astype(jnp.bfloat16)
    shares = share(0 if first else 1)
    loads[2].wait()
    width = down_buf.shape[1]
    tile = math.gcd(width, OUT_TILE)
    for low in range(0, width, tile):
        part = jnp.dot(hidden, down_buf[:, low : low + tile], preferred_element_type=jnp.float32)
        given[:, low : low + tile] = (part * shares).astype(given.dtype)
    if not first:
        for p in range(2 * blocks):
            at = 5 * (p // 2) + 2 * (p % 2)
            place = slice(p * slots, (p + 1) * slots)
            rows = jnp.concatenate([earlier_given[place, :], given[place, :]])
            back = lax.dot_general(
                pick(p), rows, (((0,), (0,)), ((), ())), preferred_element_type=jnp.float32
            ).astype(jnp.bfloat16)
            outgoing[at][...] = back[:tokens]
            if p % 2 == 0:
                outgoing[at + 1][...] = back[tokens:]
            else:
                outgoing[at + 1][...] = back[tokens : tokens + half]
                outgoing[at + 2][...] = back[tokens + half :]


def feed(first, inputs, slot_of, gates, slots, weights, extra, rows, waits=()):
    width, ff = weights[0].shape
    blocks = slot_of.shape[0]
    slots = 4 * blocks * slots

    def whole(shape):
        return pl.BlockSpec(shape, lambda i: (0,) * len(shape))

    shapes = ([(rows, width)] * 3 + [(rows // 2, width), (rows - rows // 2, width)]) * blocks
    operands = [*inputs, slot_of, gates, *weights, *extra]
    specs = [whole(v.shape) for v in operands]
    at = len(inputs) + 2
    specs[at : at + 3] = [pl.BlockSpec(memory_space=pl.ANY)] * 3
    specs += [pl.BlockSpec(memory_space=pl.ANY)] * len(waits)
    results = [(slots, width)] * 2 if first else shapes
    kept = pltpu.VMEM((slots, width), jnp.bfloat16)
    return pl.pallas_call(
        functools.partial(feed_kernel, blocks=blocks, first=first, waits=len(waits)),
        grid=(1,),
        in_specs=specs,
        out_specs=[whole(s) for s in results],
        out_shape=[jax.ShapeDtypeStruct(s, jnp.bfloat16) for s in results],
        scratch_shapes=[kept]
        + [pltpu.VMEM(w.shape, w.dtype) for w in weights]
        + [pltpu.SemaphoreType.DMA((3,))],
        compiler_params=pltpu.CompilerParams(vmem_limit_bytes=VMEM_BYTES),
        cost_estimate=pl.CostEstimate(
            flops=6 * slots * width * ff,
            bytes_accessed=6 * width * ff + 12 * blocks * rows * width,
            transcendentals=slots * ff,
        ),
        name="feed_first" if first else "feed_second",
    )(*operands, *waits)


def collect_near(own, by_x, by_y, from_a, from_b, *waits):
    half = from_a.shape[0]
    if waits:
        by_x, by_y = hold([by_x, by_y], *waits)
    by_y = jnp.concatenate([by_y[:half] + from_a, by_y[half:]])
    by_x = jnp.concatenate([by_x[:half], by_x[half:] + from_b])
    return own, swap_x(by_x), swap_y(by_y)


def add_up(parts):
    return sum(part.astype(jnp.float32) for part in parts)


def routing(ids, gates, expert_count, waits):
    dev_size = lax.axis_size("dev")
    planes = dev_size // 2
    named = ids.T[None] == jnp.arange(expert_count, dtype=jnp.int32)[:, None, None]
    [dense] = hold([jnp.sum(jnp.where(named, gates.T[None], 0.0), axis=1)], *waits)
    pair = jnp.stack([dense, swap_x(dense)])
    four = jnp.concatenate([pair, swap_y(pair)])
    every = jnp.stack([four] + [turn(four, k) for k in range(1, planes)])
    me = lax.axis_index("grp") * dev_size + lax.axis_index("dev")
    mine = jnp.stack(
        [lax.dynamic_index_in_dim(every, e, 2, keepdims=False) for e in (me, me ^ 1)], axis=1
    )
    named = mine > 0
    tokens = mine.shape[-1]
    before = jnp.triu(jnp.ones((tokens, tokens), jnp.bfloat16), 1)
    rank = jnp.dot(named.astype(jnp.bfloat16), before, preferred_element_type=jnp.float32)
    return jnp.where(named, rank, -1.0).astype(jnp.int32), mine, (pair, four)


def shards(
    queries,
    keys,
    values,
    doc_ids,
    out_weight,
    norm_gain,
    expert_ids,
    gate_values,
    expert_gate,
    expert_up,
    expert_down,
):
    own_rows = queries.shape[0]
    grp_size = lax.axis_size("grp")
    dev_size = lax.axis_size("dev")
    planes = dev_size // 2
    group, device = lax.axis_index("grp"), lax.axis_index("dev")
    dev_rows = own_rows // grp_size
    width = out_weight.shape[1]
    top_count = expert_ids.shape[2]
    expert_count = grp_size * dev_size
    capacity = max(2, 3 * dev_rows * top_count // (2 * expert_count))
    slots = -(-capacity // 16) * 16
    doc_reach = dev_size * own_rows // 2 + own_rows
    reach = min(dev_size - 1, (doc_reach + own_rows - 1) // own_rows)

    pieces = gather_keys(keys, values, reach)
    own_low = (len(pieces) - 2 + device % 2) * own_rows
    own_docs = lax.dynamic_slice_in_dim(doc_ids, device * own_rows, own_rows, 0)
    starts = jnp.sum((doc_ids[None, :] < own_docs[:, None]).astype(jnp.int32), axis=1)
    starts = starts - device * own_rows + own_low
    ends = jnp.stack([starts[::dev_rows], starts[dev_rows - 1 :: dev_rows]], axis=1)
    bounds = jnp.concatenate([jnp.stack([own_low, group, device % 2]), ends.reshape(-1)]).astype(jnp.int32)

    slot_of, gates, steps = routing(expert_ids[0], gate_values[0], expert_count, pieces[-2:])
    own_weights = [expert_gate[0], expert_up[0], expert_down[0]]
    other_weights = [swap_core(w) for w in own_weights]

    def part(mask, *waits):
        attended = attend(mask, queries, pieces, starts, bounds, dev_rows, waits)
        return jnp.dot(attended, out_weight, preferred_element_type=jnp.float32)

    half = dev_rows // 2
    far = part(3).astype(jnp.bfloat16)
    from_a, from_b = swap_x(far[:half]), swap_y(far[half:])
    by_x = part(1, far, steps[0]).astype(jnp.bfloat16)
    by_y = part(2, by_x, steps[1], *other_weights).astype(jnp.bfloat16)
    own = part(0, slot_of, gates, from_a, from_b)
    projected = add_up(collect_near(own, by_x, by_y, from_a, from_b))
    normed = (
        projected
        * lax.rsqrt(jnp.mean(projected * projected, axis=-1, keepdims=True) + 1e-06)
        * norm_gain
    ).astype(jnp.bfloat16)

    order = list(range(planes))
    turned = order[1:] + order[:1]
    sets = [turned[i : i + 2] for i in range(0, planes, 2)]
    blocks, done = {}, {}

    def feed_first(members, *waits):
        routes = [jnp.stack([part[k] for k in members]) for part in (slot_of, gates)]
        inputs = [b for k in members for b in blocks[k]]
        results = feed(True, inputs, *routes, slots, own_weights, [], dev_rows, waits)
        return members, routes, *results

    def feed_second(state, *waits):
        members, routes, given, other = state
        out = feed(False, [], *routes, slots, other_weights, [other, given], dev_rows, waits)
        for i, k in enumerate(members):
            done[k] = out[5 * i : 5 * i + 5]
        return out[0]

    def relay(near, *waits):
        first, second = halves(*near, *waits) if waits else (near[0][:half], near[1][half:])
        return swap_y(first), swap_x(second)

    near, sent, fars = (), [], [(), ()]

    def launch(k):
        nonlocal near
        block = normed
        if k:
            block = jnp.copy(normed)
            if len(sent) > 1:
                [block] = hold([block], *sent[-2])
            [block] = hold([turn(block, k)], *near, *fars[-2])
        near = swap_x(block), swap_y(block)
        blocks[k] = [block]

    def relay(k, *waits):
        nonlocal near
        near = hold(near, *waits) if waits else near
        sent.append((near[0][:half], near[1][half:]))
        far = swap_y(sent[-1][0]), swap_x(sent[-1][1])
        fars.append(far)
        blocks[k] += [*near, *far]
        return far

    launch(0)
    far = relay(0)
    for i, members in enumerate(sets[:-1]):
        for k in members:
            if k not in blocks:
                launch(k)
                relay(k)
        following = next(k for k in sets[i + 1] if k)
        state = feed_first(members)
        launch(following)
        far = relay(following, state[2])
        feed_second(state, *near)

    early = [k for members in sets[:-1][::-1] for k in members[::-1]]
    late = [k for k in sets[-1] if k] + [0]
    froms, sums = {}, []

    def far_part(k):
        froms[k] = swap_x(done[k][3]), swap_y(done[k][4])
        return froms[k]

    def near_part(k, *waits):
        parts = collect_near(*done[k][:3], *froms[k], *waits)
        summed = add_up(parts)
        if k:
            summed = turn(summed.astype(jnp.bfloat16), planes - k).astype(jnp.float32)
        sums.append(summed)
        return parts[1:]

    def held(k, *waits):
        done[k] = [*done[k][:3], *hold(done[k][3:5], *waits)]

    chain = far
    for k in early[:1]:
        held(k, *chain)
        chain = far_part(k)
    state = feed_first(sets[-1], *chain)
    arrived = ()
    for k in early[:1]:
        arrived = near_part(k)
    for k in early[1:]:
        held(k, *chain)
        chain = far_part(k)
    feed_second(state, *arrived, *chain)
    for k in early[1:]:
        arrived = near_part(k, state[2])
    chain = arrived
    for k in late:
        held(k, *chain)
        chain = far_part(k)
        near_part(k)
    return (projected + sum(sums)).astype(jnp.bfloat16)[None]


def solution(mesh):
    return jax.shard_map(
        shards,
        mesh=mesh,
        in_specs=(
            P("dev", "grp"),
            P("dev", "grp"),
            P("dev", "grp"),
            P(),
            P("grp", None),
            P(),
            P("dev", "grp", None),
            P("dev", "grp", None),
            P(("grp", "dev"), None, None),
            P(("grp", "dev"), None, None),
            P(("grp", "dev"), None, None),
        ),
        out_specs=P("dev", "grp", None),
        check_vma=False,
    )
```

```python
import functools
import math

import jax
import jax.numpy as jnp
from jax import lax
from jax.experimental import pallas as pl
from jax.experimental.pallas import tpu as pltpu
from jax.sharding import PartitionSpec as P

HEAD_SIZE = 128
KEY_BLOCK = 512
SPLIT = 8
IN_TILE = 256
OUT_TILE = 512
VMEM_BYTES = 56 * 1024 * 1024
LOW = -1e30


def after(value, *others):
    return lax.optimization_barrier((value, *others))[0]


def swap_x(value):
    return lax.ppermute(value, "grp", [(i, i ^ 1) for i in range(lax.axis_size("grp"))])


def swap_y(value):
    return lax.ppermute(value, "grp", [(i, i ^ 2) for i in range(lax.axis_size("grp"))])


def swap_core(value):
    return lax.ppermute(value, "dev", [(i, i ^ 1) for i in range(lax.axis_size("dev"))])


def turn(value, planes):
    count = lax.axis_size("dev")
    return lax.ppermute(value, "dev", [(i, (i - 2 * planes) % count) for i in range(count)])


def earlier(value, steps, sources=lambda source: True):
    count = lax.axis_size("dev")
    pairs = [(i, i + steps) for i in range(count - steps) if sources(i)]
    return lax.ppermute(value, "dev", pairs)


def hold_kernel(*refs):
    del refs


def hold(values, *waits):
    anywhere = pl.BlockSpec(memory_space=pl.ANY)
    return pl.pallas_call(
        hold_kernel,
        in_specs=[anywhere] * (len(values) + len(waits)),
        out_specs=[anywhere] * len(values),
        out_shape=[jax.ShapeDtypeStruct(v.shape, v.dtype) for v in values],
        input_output_aliases={i: i for i in range(len(values))},
        cost_estimate=pl.CostEstimate(flops=0, bytes_accessed=0, transcendentals=0),
        name="hold",
    )(*values, *waits)


def gather_keys(keys, values, reach):
    own = jnp.concatenate([keys, values], axis=1)
    whole = reach // 2
    lanes = [own]
    for _ in range(whole):
        lanes.append(earlier(lanes[-1], 2))
    pieces = [piece for lane in lanes[::-1] for piece in (lane, swap_core(lane))]
    if reach % 2:
        pieces = [earlier(own, reach, lambda source: source % 2 == 1)] + pieces
    return pieces


def attend_kernel(bounds, *refs, shards, waits, mask):
    q_ref, start_ref = refs[:2]
    pieces = refs[2 : 2 + shards]
    out_ref, q_all, kv_ref, top, total = refs[2 + shards + waits :]
    size = pieces[0].shape[0]
    core = bounds[2]
    for i, piece in enumerate(pieces):
        lone = shards % 2
        if i < lone:
            at = 0
        else:
            pair = i - (i - lone) % 2
            at = pair + (core if pair == i else 1 - core)
        kv_ref[pl.ds(pl.multiple_of(at * size, size), size), :] = piece[...]
    rows = q_ref.shape[0]
    heads = q_ref.shape[1] // HEAD_SIZE
    for h in range(heads):
        q_all[h * rows : (h + 1) * rows, :] = q_ref[:, h * HEAD_SIZE : (h + 1) * HEAD_SIZE]
    top[...] = jnp.full_like(top, LOW)
    total[...] = jnp.zeros_like(total)
    block_index = bounds[1] ^ mask
    q_low = bounds[0] + block_index * rows
    first_start, last_start = bounds[3 + 2 * block_index], bounds[4 + 2 * block_index]
    factor = math.log2(math.e) / math.sqrt(HEAD_SIZE)

    def step(block, masked):
        low = pl.multiple_of(block * KEY_BLOCK, KEY_BLOCK)
        key = kv_ref[pl.ds(low, KEY_BLOCK), :HEAD_SIZE]
        value = kv_ref[pl.ds(low, KEY_BLOCK), HEAD_SIZE:]
        value = jnp.concatenate([value, jnp.ones_like(value)], axis=1)
        if masked:
            key_pos = low + lax.broadcasted_iota(jnp.int32, (rows, KEY_BLOCK), 1)
            q_pos = q_low + lax.broadcasted_iota(jnp.int32, (rows, KEY_BLOCK), 0)
            seen = (key_pos >= start_ref[...]) & (key_pos <= q_pos)
        part_heads = heads // SPLIT
        size = part_heads * rows
        scores = []
        for r in range(SPLIT):
            scores.append(lax.dot_general(
                q_all[r * size : (r + 1) * size, :], key, (((1,), (1,)), ((), ())), preferred_element_type=jnp.float32
            ))
        for r in range(SPLIT):
            span = slice(r * size, (r + 1) * size)
            score = scores[r] * factor
            if masked:
                score = jnp.where(seen[None], score.reshape(part_heads, rows, KEY_BLOCK), LOW)
                score = score.reshape(size, KEY_BLOCK)
            old = top[span, :]
            new = jnp.maximum(old, jnp.max(score, axis=1, keepdims=True))
            weight = jnp.exp2(score - jnp.concatenate([new] * (KEY_BLOCK // HEAD_SIZE), axis=1))
            shrink = jnp.exp2(old - new)
            added = jnp.dot(weight.astype(jnp.bfloat16), value, preferred_element_type=jnp.float32)
            total[span, :] = total[span, :] * jnp.concatenate([shrink, shrink], axis=1) + added
            top[span, :] = new

    def loop(low, high, masked):
        def body(block, carry):
            step(block, masked)
            return carry

        lax.fori_loop(low, high, body, 0)

    begin = first_start // KEY_BLOCK
    end = (q_low + rows - 1) // KEY_BLOCK + 1
    inner_low = jnp.minimum((last_start + KEY_BLOCK - 1) // KEY_BLOCK, end)
    inner_high = jnp.maximum((q_low + 1) // KEY_BLOCK, inner_low)
    loop(begin, inner_low, True)
    loop(inner_low, inner_high, False)
    loop(inner_high, end, True)
    for h in range(heads):
        part = total[h * rows : (h + 1) * rows, :]
        out_ref[:, h * HEAD_SIZE : (h + 1) * HEAD_SIZE] = (
            part[:, :HEAD_SIZE] / part[:, HEAD_SIZE:]
        ).astype(out_ref.dtype)


def attend(mask, queries, pieces, starts, bounds, rows, waits=()):
    width = queries.shape[1]
    heads = width // HEAD_SIZE
    length = len(pieces) * pieces[0].shape[0]
    pairs = heads * rows * length // 2
    return pl.pallas_call(
        functools.partial(attend_kernel, shards=len(pieces), waits=len(waits), mask=mask),
        grid_spec=pltpu.PrefetchScalarGridSpec(
            num_scalar_prefetch=1,
            grid=(1,),
            in_specs=[
                pl.BlockSpec((rows, width), lambda i, bounds: (bounds[1] ^ mask, 0)),
                pl.BlockSpec((rows, 1), lambda i, bounds: (bounds[1] ^ mask, 0)),
            ]
            + [pl.BlockSpec(p.shape, lambda i, bounds: (0, 0)) for p in pieces]
            + [pl.BlockSpec(memory_space=pl.ANY)] * len(waits),
            out_specs=pl.BlockSpec((rows, width), lambda i, bounds: (0, 0)),
            scratch_shapes=[
                pltpu.VMEM((heads * rows, HEAD_SIZE), jnp.bfloat16),
                pltpu.VMEM((length, 2 * HEAD_SIZE), jnp.bfloat16),
                pltpu.VMEM((heads * rows, HEAD_SIZE), jnp.float32),
                pltpu.VMEM((heads * rows, 2 * HEAD_SIZE), jnp.float32),
            ],
        ),
        out_shape=jax.ShapeDtypeStruct((rows, width), jnp.bfloat16),
        compiler_params=pltpu.CompilerParams(vmem_limit_bytes=VMEM_BYTES),
        cost_estimate=pl.CostEstimate(
            flops=4 * pairs * HEAD_SIZE, bytes_accessed=4 * length * HEAD_SIZE, transcendentals=pairs
        ),
        name="attend",
    )(bounds, queries, starts[:, None], *pieces, *waits)


def feed_kernel(*refs, blocks, first, waits):
    refs = list(refs)
    gates_kept, hidden, gate_buf, up_buf, down_buf, sems = refs[-6:]
    del refs[-6:]
    incoming = [refs.pop(0) for _ in range(5 * blocks)] if first else None
    slot_of, gates, gate_ref, up_ref, down_ref = (refs.pop(0) for _ in range(5))
    if not first:
        taken, earlier_given = refs.pop(0), refs.pop(0)
    refs = refs[waits:]
    if first:
        given, other, taken = refs
    else:
        outgoing, given = refs[: 5 * blocks], refs[5 * blocks]
    loads = [
        pltpu.make_async_copy(source, target, sems.at[i])
        for i, (source, target) in enumerate(
            ((gate_ref, gate_buf), (up_ref, up_buf), (down_ref, down_buf))
        )
    ]
    for load in loads:
        load.start()
    tokens = slot_of.shape[3]
    half = tokens // 2
    slots = given.shape[0] // (2 * blocks)
    each = slots // 2

    def chosen(p, e, b):
        at = 2 * p + b
        mine = slot_of[at // 4, e, at % 4 : at % 4 + 1, :]
        return lax.broadcasted_iota(jnp.int32, (each, tokens), 0) == mine

    def pick(p):
        lines = []
        for e in range(2):
            for b in range(2):
                found = chosen(p, e, b).astype(jnp.float32)
                zeros = jnp.zeros_like(found)
                lines.append(jnp.concatenate([zeros, found] if b else [found, zeros], axis=1))
        return jnp.concatenate(lines).astype(jnp.bfloat16)

    def share(e):
        parts = []
        for p in range(2 * blocks):
            for b in range(2):
                at = 2 * p + b
                gate = gates[at // 4, e, at % 4 : at % 4 + 1, :]
                parts.append(jnp.sum(jnp.where(chosen(p, e, b), gate, 0.0), axis=1, keepdims=True))
        return jnp.concatenate(parts)

    if first:
        for p in range(2 * blocks):
            at = 5 * (p // 2) + 2 * (p % 2)
            held = jnp.concatenate([piece[...] for piece in incoming[at : at + 2 + p % 2]])
            found = jnp.dot(pick(p), held, preferred_element_type=jnp.float32).astype(taken.dtype)
            taken[p * slots : (p + 1) * slots, :] = found[:slots]
            other[p * slots : (p + 1) * slots, :] = found[slots:]

    ff, width = down_buf.shape
    inner, outer = math.gcd(ff, IN_TILE), math.gcd(width, OUT_TILE)

    def tiles(count, body):
        lax.fori_loop(0, count, lambda i, carry: (body(i), carry)[1], 0)

    def gate_tile(i):
        at = pl.ds(pl.multiple_of(i * inner, inner), inner)
        gate = jnp.dot(taken[...], gate_buf[:, at], preferred_element_type=jnp.float32)
        gates_kept[:, at] = gate / (1.0 + jnp.exp(-gate))

    def up_tile(i):
        at = pl.ds(pl.multiple_of(i * inner, inner), inner)
        up = jnp.dot(taken[...], up_buf[:, at], preferred_element_type=jnp.float32)
        hidden[:, at] = (gates_kept[:, at] * up).astype(jnp.bfloat16)

    def down_tile(i):
        at = pl.ds(pl.multiple_of(i * outer, outer), outer)
        part = jnp.dot(hidden[...], down_buf[:, at], preferred_element_type=jnp.float32)
        given[:, at] = (part * shares).astype(given.dtype)

    loads[0].wait()
    tiles(ff // inner, gate_tile)
    loads[1].wait()
    tiles(ff // inner, up_tile)
    shares = share(0 if first else 1)
    loads[2].wait()
    tiles(width // outer, down_tile)
    if not first:
        for p in range(2 * blocks):
            at = 5 * (p // 2) + 2 * (p % 2)
            place = slice(p * slots, (p + 1) * slots)
            rows = jnp.concatenate([earlier_given[place, :], given[place, :]])
            back = lax.dot_general(
                pick(p), rows, (((0,), (0,)), ((), ())), preferred_element_type=jnp.float32
            ).astype(jnp.bfloat16)
            outgoing[at][...] = back[:tokens]
            if p % 2 == 0:
                outgoing[at + 1][...] = back[tokens:]
            else:
                outgoing[at + 1][...] = back[tokens : tokens + half]
                outgoing[at + 2][...] = back[tokens + half :]


def feed(first, inputs, slot_of, gates, slots, weights, extra, rows, waits=()):
    width, ff = weights[0].shape
    blocks = slot_of.shape[0]
    slots = 4 * blocks * slots

    def whole(shape):
        return pl.BlockSpec(shape, lambda i: (0,) * len(shape))

    shapes = ([(rows, width)] * 3 + [(rows // 2, width), (rows - rows // 2, width)]) * blocks
    operands = [*inputs, slot_of, gates, *weights, *extra]
    specs = [whole(v.shape) for v in operands]
    at = len(inputs) + 2
    specs[at : at + 3] = [pl.BlockSpec(memory_space=pl.ANY)] * 3
    specs += [pl.BlockSpec(memory_space=pl.ANY)] * len(waits)
    results = [(slots, width)] * 2 if first else shapes
    kept = pltpu.VMEM((slots, width), jnp.bfloat16)
    return pl.pallas_call(
        functools.partial(feed_kernel, blocks=blocks, first=first, waits=len(waits)),
        grid=(1,),
        in_specs=specs,
        out_specs=[whole(s) for s in results],
        out_shape=[jax.ShapeDtypeStruct(s, jnp.bfloat16) for s in results],
        scratch_shapes=[
            kept,
            pltpu.VMEM((slots, ff), jnp.float32),
            pltpu.VMEM((slots, ff), jnp.bfloat16),
        ]
        + [pltpu.VMEM(w.shape, w.dtype) for w in weights]
        + [pltpu.SemaphoreType.DMA((3,))],
        compiler_params=pltpu.CompilerParams(vmem_limit_bytes=VMEM_BYTES),
        cost_estimate=pl.CostEstimate(
            flops=6 * slots * width * ff,
            bytes_accessed=6 * width * ff + 12 * blocks * rows * width,
            transcendentals=slots * ff,
        ),
        name="feed_first" if first else "feed_second",
    )(*operands, *waits)


def collect_near(own, by_x, by_y, from_a, from_b, *waits):
    half = from_a.shape[0]
    if waits:
        by_x, by_y = hold([by_x, by_y], *waits)
    by_y = jnp.concatenate([by_y[:half] + from_a, by_y[half:]])
    by_x = jnp.concatenate([by_x[:half], by_x[half:] + from_b])
    return own, swap_x(by_x), swap_y(by_y)


def add_up(parts):
    return sum(part.astype(jnp.float32) for part in parts)


def routing(ids, gates, expert_count, waits):
    dev_size = lax.axis_size("dev")
    planes = dev_size // 2
    named = ids.T[None] == jnp.arange(expert_count, dtype=jnp.int32)[:, None, None]
    [dense] = hold([jnp.sum(jnp.where(named, gates.T[None], 0.0), axis=1)], *waits)
    pair = jnp.stack([dense, swap_x(dense)])
    four = jnp.concatenate([pair, swap_y(pair)])
    every = jnp.stack([four] + [turn(four, k) for k in range(1, planes)])
    me = lax.axis_index("grp") * dev_size + lax.axis_index("dev")
    mine = jnp.stack(
        [lax.dynamic_index_in_dim(every, e, 2, keepdims=False) for e in (me, me ^ 1)], axis=1
    )
    named = mine > 0
    tokens = mine.shape[-1]
    before = jnp.triu(jnp.ones((tokens, tokens), jnp.bfloat16), 1)
    rank = jnp.dot(named.astype(jnp.bfloat16), before, preferred_element_type=jnp.float32)
    return jnp.where(named, rank, -1.0).astype(jnp.int32), mine, (pair, four)


def shards(
    queries,
    keys,
    values,
    doc_ids,
    out_weight,
    norm_gain,
    expert_ids,
    gate_values,
    expert_gate,
    expert_up,
    expert_down,
):
    own_rows = queries.shape[0]
    grp_size = lax.axis_size("grp")
    dev_size = lax.axis_size("dev")
    planes = dev_size // 2
    group, device = lax.axis_index("grp"), lax.axis_index("dev")
    dev_rows = own_rows // grp_size
    width = out_weight.shape[1]
    top_count = expert_ids.shape[2]
    expert_count = grp_size * dev_size
    capacity = max(2, 3 * dev_rows * top_count // (2 * expert_count))
    slots = -(-capacity // 16) * 16
    doc_reach = dev_size * own_rows // 2 + own_rows
    reach = min(dev_size - 1, (doc_reach + own_rows - 1) // own_rows)

    pieces = gather_keys(keys, values, reach)
    own_low = (len(pieces) - 2 + device % 2) * own_rows
    own_docs = lax.dynamic_slice_in_dim(doc_ids, device * own_rows, own_rows, 0)
    starts = jnp.sum((doc_ids[None, :] < own_docs[:, None]).astype(jnp.int32), axis=1)
    starts = starts - device * own_rows + own_low
    ends = jnp.stack([starts[::dev_rows], starts[dev_rows - 1 :: dev_rows]], axis=1)
    bounds = jnp.concatenate([jnp.stack([own_low, group, device % 2]), ends.reshape(-1)]).astype(jnp.int32)

    slot_of, gates, steps = routing(expert_ids[0], gate_values[0], expert_count, pieces[-2:])
    own_weights = [expert_gate[0], expert_up[0], expert_down[0]]
    other_weights = [swap_core(w) for w in own_weights]

    def part(mask, *waits):
        attended = attend(mask, queries, pieces, starts, bounds, dev_rows, waits)
        return jnp.dot(attended, out_weight, preferred_element_type=jnp.float32)

    half = dev_rows // 2
    far = part(3).astype(jnp.bfloat16)
    from_a, from_b = swap_x(far[:half]), swap_y(far[half:])
    by_x = part(1, far, steps[0]).astype(jnp.bfloat16)
    by_y = part(2, by_x, steps[1], *other_weights).astype(jnp.bfloat16)
    own = part(0, slot_of, gates, from_a, from_b)
    projected = add_up(collect_near(own, by_x, by_y, from_a, from_b))
    normed = (
        projected
        * lax.rsqrt(jnp.mean(projected * projected, axis=-1, keepdims=True) + 1e-06)
        * norm_gain
    ).astype(jnp.bfloat16)

    order = list(range(planes))
    turned = order[1:] + order[:1]
    sets = [turned[i : i + 2] for i in range(0, planes, 2)]
    blocks, done = {}, {}

    def feed_first(members, *waits):
        routes = [jnp.stack([part[k] for k in members]) for part in (slot_of, gates)]
        inputs = [b for k in members for b in blocks[k]]
        results = feed(True, inputs, *routes, slots, own_weights, [], dev_rows, waits)
        return members, routes, *results

    def feed_second(state, *waits):
        members, routes, given, other = state
        out = feed(False, [], *routes, slots, other_weights, [other, given], dev_rows, waits)
        for i, k in enumerate(members):
            done[k] = out[5 * i : 5 * i + 5]
        return out[0]

    def relay(near, *waits):
        first, second = halves(*near, *waits) if waits else (near[0][:half], near[1][half:])
        return swap_y(first), swap_x(second)

    near, sent, fars = (), [], [(), ()]

    def launch(k):
        nonlocal near
        block = normed
        if k:
            block = jnp.copy(normed)
            if len(sent) > 1:
                [block] = hold([block], *sent[-2])
            [block] = hold([turn(block, k)], *near, *fars[-2])
        near = swap_x(block), swap_y(block)
        blocks[k] = [block]

    def relay(k, *waits):
        nonlocal near
        near = hold(near, *waits) if waits else near
        sent.append((near[0][:half], near[1][half:]))
        far = swap_y(sent[-1][0]), swap_x(sent[-1][1])
        fars.append(far)
        blocks[k] += [*near, *far]
        return far

    launch(0)
    far = relay(0)
    for i, members in enumerate(sets[:-1]):
        for k in members:
            if k not in blocks:
                launch(k)
                relay(k)
        following = next(k for k in sets[i + 1] if k)
        state = feed_first(members)
        launch(following)
        far = relay(following, state[2])
        feed_second(state, *near)

    early = [k for members in sets[:-1][::-1] for k in members[::-1]]
    late = [k for k in sets[-1] if k] + [0]
    froms, sums = {}, []

    def far_part(k):
        froms[k] = swap_x(done[k][3]), swap_y(done[k][4])
        return froms[k]

    def near_part(k, *waits):
        parts = collect_near(*done[k][:3], *froms[k], *waits)
        summed = add_up(parts)
        if k:
            summed = turn(summed.astype(jnp.bfloat16), planes - k).astype(jnp.float32)
        sums.append(summed)
        return parts[1:]

    def held(k, *waits):
        done[k] = [*done[k][:3], *hold(done[k][3:5], *waits)]

    chain = far
    for k in early[:1]:
        held(k, *chain)
        chain = far_part(k)
    state = feed_first(sets[-1], *chain)
    arrived = ()
    for k in early[:1]:
        arrived = near_part(k)
    for k in early[1:]:
        held(k, *chain)
        chain = far_part(k)
    feed_second(state, *arrived, *chain)
    for k in early[1:]:
        arrived = near_part(k, state[2])
    chain = arrived
    for k in late:
        held(k, *chain)
        chain = far_part(k)
        near_part(k)
    return (projected + sum(sums)).astype(jnp.bfloat16)[None]


def solution(mesh):
    return jax.shard_map(
        shards,
        mesh=mesh,
        in_specs=(
            P("dev", "grp"),
            P("dev", "grp"),
            P("dev", "grp"),
            P(),
            P("grp", None),
            P(),
            P("dev", "grp", None),
            P("dev", "grp", None),
            P(("grp", "dev"), None, None),
            P(("grp", "dev"), None, None),
            P(("grp", "dev"), None, None),
        ),
        out_specs=P("dev", "grp", None),
        check_vma=False,
    )
```

```python
import functools
import math

import jax
import jax.numpy as jnp
from jax import lax
from jax.experimental import pallas as pl
from jax.experimental.pallas import tpu as pltpu
from jax.sharding import PartitionSpec as P

HEAD_SIZE = 128
KEY_BLOCK = 512
SPLIT = 8
IN_TILE = 256
OUT_TILE = 512
VMEM_BYTES = 56 * 1024 * 1024
LOW = -1e30


def after(value, *others):
    return lax.optimization_barrier((value, *others))[0]


def swap_grp(value, even, odd):
    grp_size, dev_size = lax.axis_size("grp"), lax.axis_size("dev")
    pairs = [
        (g * dev_size + d, (g ^ (odd if d % 2 else even)) * dev_size + d)
        for g in range(grp_size)
        for d in range(dev_size)
    ]
    return lax.ppermute(value, ("grp", "dev"), pairs)


def swap_x(value):
    return swap_grp(value, 1, 2)


def swap_y(value):
    return swap_grp(value, 2, 1)


def swap_core(value):
    return lax.ppermute(value, "dev", [(i, i ^ 1) for i in range(lax.axis_size("dev"))])


def turn(value, planes):
    count = lax.axis_size("dev")
    return lax.ppermute(value, "dev", [(i, (i - 2 * planes) % count) for i in range(count)])


def earlier(value, steps, sources=lambda source: True):
    count = lax.axis_size("dev")
    pairs = [(i, i + steps) for i in range(count - steps) if sources(i)]
    return lax.ppermute(value, "dev", pairs)


def hold_kernel(*refs):
    del refs


def hold(values, *waits):
    anywhere = pl.BlockSpec(memory_space=pl.ANY)
    return pl.pallas_call(
        hold_kernel,
        in_specs=[anywhere] * (len(values) + len(waits)),
        out_specs=[anywhere] * len(values),
        out_shape=[jax.ShapeDtypeStruct(v.shape, v.dtype) for v in values],
        input_output_aliases={i: i for i in range(len(values))},
        cost_estimate=pl.CostEstimate(flops=0, bytes_accessed=0, transcendentals=0),
        name="hold",
    )(*values, *waits)


def gather_keys(keys, values, reach):
    own = jnp.concatenate([keys, values], axis=1)
    whole = reach // 2
    lanes = [own]
    for _ in range(whole):
        lanes.append(earlier(lanes[-1], 2))
    pieces = [piece for lane in lanes[::-1] for piece in (lane, swap_core(lane))]
    if reach % 2:
        pieces = [earlier(own, reach, lambda source: source % 2 == 1)] + pieces
    return pieces


def attend_kernel(bounds, *refs, shards, waits, role):
    q_ref, start_ref = refs[:2]
    pieces = refs[2 : 2 + shards]
    out_ref, q_all, kv_ref, top, total = refs[2 + shards + waits :]
    size = pieces[0].shape[0]
    core = bounds[4]
    for i, piece in enumerate(pieces):
        lone = shards % 2
        if i < lone:
            at = 0
        else:
            pair = i - (i - lone) % 2
            at = pair + (core if pair == i else 1 - core)
        kv_ref[pl.ds(pl.multiple_of(at * size, size), size), :] = piece[...]
    rows = q_ref.shape[0]
    heads = q_ref.shape[1] // HEAD_SIZE
    for h in range(heads):
        q_all[h * rows : (h + 1) * rows, :] = q_ref[:, h * HEAD_SIZE : (h + 1) * HEAD_SIZE]
    top[...] = jnp.full_like(top, LOW)
    total[...] = jnp.zeros_like(total)
    block_index = bounds[role]
    q_low = bounds[0] + block_index * rows
    first_start, last_start = bounds[6 + 2 * block_index], bounds[7 + 2 * block_index]
    factor = math.log2(math.e) / math.sqrt(HEAD_SIZE)

    def step(block, masked):
        low = pl.multiple_of(block * KEY_BLOCK, KEY_BLOCK)
        key = kv_ref[pl.ds(low, KEY_BLOCK), :HEAD_SIZE]
        value = kv_ref[pl.ds(low, KEY_BLOCK), HEAD_SIZE:]
        value = jnp.concatenate([value, jnp.ones_like(value)], axis=1)
        if masked:
            key_pos = low + lax.broadcasted_iota(jnp.int32, (rows, KEY_BLOCK), 1)
            q_pos = q_low + lax.broadcasted_iota(jnp.int32, (rows, KEY_BLOCK), 0)
            seen = (key_pos >= start_ref[...]) & (key_pos <= q_pos)
        part_heads = heads // SPLIT
        size = part_heads * rows
        scores = []
        for r in range(SPLIT):
            scores.append(lax.dot_general(
                q_all[r * size : (r + 1) * size, :], key, (((1,), (1,)), ((), ())), preferred_element_type=jnp.float32
            ))
        for r in range(SPLIT):
            span = slice(r * size, (r + 1) * size)
            score = scores[r] * factor
            if masked:
                score = jnp.where(seen[None], score.reshape(part_heads, rows, KEY_BLOCK), LOW)
                score = score.reshape(size, KEY_BLOCK)
            old = top[span, :]
            new = jnp.maximum(old, jnp.max(score, axis=1, keepdims=True))
            weight = jnp.exp2(score - jnp.concatenate([new] * (KEY_BLOCK // HEAD_SIZE), axis=1))
            shrink = jnp.exp2(old - new)
            added = jnp.dot(weight.astype(jnp.bfloat16), value, preferred_element_type=jnp.float32)
            total[span, :] = total[span, :] * jnp.concatenate([shrink, shrink], axis=1) + added
            top[span, :] = new

    def loop(low, high, masked):
        def body(block, carry):
            step(block, masked)
            return carry

        lax.fori_loop(low, high, body, 0)

    begin = first_start // KEY_BLOCK
    end = (q_low + rows - 1) // KEY_BLOCK + 1
    inner_low = jnp.minimum((last_start + KEY_BLOCK - 1) // KEY_BLOCK, end)
    inner_high = jnp.maximum((q_low + 1) // KEY_BLOCK, inner_low)
    loop(begin, inner_low, True)
    loop(inner_low, inner_high, False)
    loop(inner_high, end, True)
    for h in range(heads):
        part = total[h * rows : (h + 1) * rows, :]
        out_ref[:, h * HEAD_SIZE : (h + 1) * HEAD_SIZE] = (
            part[:, :HEAD_SIZE] / part[:, HEAD_SIZE:]
        ).astype(out_ref.dtype)


def attend(role, queries, pieces, starts, bounds, rows, waits=()):
    width = queries.shape[1]
    heads = width // HEAD_SIZE
    length = len(pieces) * pieces[0].shape[0]
    pairs = heads * rows * length // 2
    return pl.pallas_call(
        functools.partial(attend_kernel, shards=len(pieces), waits=len(waits), role=role),
        grid_spec=pltpu.PrefetchScalarGridSpec(
            num_scalar_prefetch=1,
            grid=(1,),
            in_specs=[
                pl.BlockSpec((rows, width), lambda i, bounds: (bounds[role], 0)),
                pl.BlockSpec((rows, 1), lambda i, bounds: (bounds[role], 0)),
            ]
            + [pl.BlockSpec(p.shape, lambda i, bounds: (0, 0)) for p in pieces]
            + [pl.BlockSpec(memory_space=pl.ANY)] * len(waits),
            out_specs=pl.BlockSpec((rows, width), lambda i, bounds: (0, 0)),
            scratch_shapes=[
                pltpu.VMEM((heads * rows, HEAD_SIZE), jnp.bfloat16),
                pltpu.VMEM((length, 2 * HEAD_SIZE), jnp.bfloat16),
                pltpu.VMEM((heads * rows, HEAD_SIZE), jnp.float32),
                pltpu.VMEM((heads * rows, 2 * HEAD_SIZE), jnp.float32),
            ],
        ),
        out_shape=jax.ShapeDtypeStruct((rows, width), jnp.bfloat16),
        compiler_params=pltpu.CompilerParams(vmem_limit_bytes=VMEM_BYTES),
        cost_estimate=pl.CostEstimate(
            flops=4 * pairs * HEAD_SIZE, bytes_accessed=4 * length * HEAD_SIZE, transcendentals=pairs
        ),
        name="attend",
    )(bounds, queries, starts[:, None], *pieces, *waits)


def feed_kernel(*refs, blocks, first, waits):
    refs = list(refs)
    gates_kept, hidden, gate_buf, up_buf, down_buf, sems = refs[-6:]
    del refs[-6:]
    incoming = [refs.pop(0) for _ in range(5 * blocks)] if first else None
    slot_of, gates, gate_ref, up_ref, down_ref = (refs.pop(0) for _ in range(5))
    if not first:
        taken, earlier_given = refs.pop(0), refs.pop(0)
    refs = refs[waits:]
    if first:
        given, other, taken = refs
    else:
        outgoing, given = refs[: 5 * blocks], refs[5 * blocks]
    loads = [
        pltpu.make_async_copy(source, target, sems.at[i])
        for i, (source, target) in enumerate(
            ((gate_ref, gate_buf), (up_ref, up_buf), (down_ref, down_buf))
        )
    ]
    for load in loads:
        load.start()
    tokens = slot_of.shape[3]
    half = tokens // 2
    slots = given.shape[0] // (2 * blocks)
    each = slots // 2

    def chosen(p, e, b):
        at = 2 * p + b
        mine = slot_of[at // 4, e, at % 4 : at % 4 + 1, :]
        return lax.broadcasted_iota(jnp.int32, (each, tokens), 0) == mine

    def pick(p):
        lines = []
        for e in range(2):
            for b in range(2):
                found = chosen(p, e, b).astype(jnp.float32)
                zeros = jnp.zeros_like(found)
                lines.append(jnp.concatenate([zeros, found] if b else [found, zeros], axis=1))
        return jnp.concatenate(lines).astype(jnp.bfloat16)

    def share(e):
        parts = []
        for p in range(2 * blocks):
            for b in range(2):
                at = 2 * p + b
                gate = gates[at // 4, e, at % 4 : at % 4 + 1, :]
                parts.append(jnp.sum(jnp.where(chosen(p, e, b), gate, 0.0), axis=1, keepdims=True))
        return jnp.concatenate(parts)

    if first:
        for p in range(2 * blocks):
            at = 5 * (p // 2) + 2 * (p % 2)
            held = jnp.concatenate([piece[...] for piece in incoming[at : at + 2 + p % 2]])
            found = jnp.dot(pick(p), held, preferred_element_type=jnp.float32).astype(taken.dtype)
            taken[p * slots : (p + 1) * slots, :] = found[:slots]
            other[p * slots : (p + 1) * slots, :] = found[slots:]

    ff, width = down_buf.shape
    inner, outer = math.gcd(ff, IN_TILE), math.gcd(width, OUT_TILE)

    def tiles(count, body):
        lax.fori_loop(0, count, lambda i, carry: (body(i), carry)[1], 0)

    def gate_tile(i):
        at = pl.ds(pl.multiple_of(i * inner, inner), inner)
        gate = jnp.dot(taken[...], gate_buf[:, at], preferred_element_type=jnp.float32)
        gates_kept[:, at] = gate / (1.0 + jnp.exp(-gate))

    def up_tile(i):
        at = pl.ds(pl.multiple_of(i * inner, inner), inner)
        up = jnp.dot(taken[...], up_buf[:, at], preferred_element_type=jnp.float32)
        hidden[:, at] = (gates_kept[:, at] * up).astype(jnp.bfloat16)

    def down_tile(i):
        at = pl.ds(pl.multiple_of(i * outer, outer), outer)
        part = jnp.dot(hidden[...], down_buf[:, at], preferred_element_type=jnp.float32)
        given[:, at] = (part * shares).astype(given.dtype)

    loads[0].wait()
    tiles(ff // inner, gate_tile)
    loads[1].wait()
    tiles(ff // inner, up_tile)
    shares = share(0 if first else 1)
    loads[2].wait()
    tiles(width // outer, down_tile)
    if not first:
        for p in range(2 * blocks):
            at = 5 * (p // 2) + 2 * (p % 2)
            place = slice(p * slots, (p + 1) * slots)
            rows = jnp.concatenate([earlier_given[place, :], given[place, :]])
            back = lax.dot_general(
                pick(p), rows, (((0,), (0,)), ((), ())), preferred_element_type=jnp.float32
            ).astype(jnp.bfloat16)
            outgoing[at][...] = back[:tokens]
            if p % 2 == 0:
                outgoing[at + 1][...] = back[tokens:]
            else:
                outgoing[at + 1][...] = back[tokens : tokens + half]
                outgoing[at + 2][...] = back[tokens + half :]


def feed(first, inputs, slot_of, gates, slots, weights, extra, rows, waits=()):
    width, ff = weights[0].shape
    blocks = slot_of.shape[0]
    slots = 4 * blocks * slots

    def whole(shape):
        return pl.BlockSpec(shape, lambda i: (0,) * len(shape))

    shapes = ([(rows, width)] * 3 + [(rows // 2, width), (rows - rows // 2, width)]) * blocks
    operands = [*inputs, slot_of, gates, *weights, *extra]
    specs = [whole(v.shape) for v in operands]
    at = len(inputs) + 2
    specs[at : at + 3] = [pl.BlockSpec(memory_space=pl.ANY)] * 3
    specs += [pl.BlockSpec(memory_space=pl.ANY)] * len(waits)
    results = [(slots, width)] * 2 if first else shapes
    kept = pltpu.VMEM((slots, width), jnp.bfloat16)
    return pl.pallas_call(
        functools.partial(feed_kernel, blocks=blocks, first=first, waits=len(waits)),
        grid=(1,),
        in_specs=specs,
        out_specs=[whole(s) for s in results],
        out_shape=[jax.ShapeDtypeStruct(s, jnp.bfloat16) for s in results],
        scratch_shapes=[
            kept,
            pltpu.VMEM((slots, ff), jnp.float32),
            pltpu.VMEM((slots, ff), jnp.bfloat16),
        ]
        + [pltpu.VMEM(w.shape, w.dtype) for w in weights]
        + [pltpu.SemaphoreType.DMA((3,))],
        compiler_params=pltpu.CompilerParams(vmem_limit_bytes=VMEM_BYTES),
        cost_estimate=pl.CostEstimate(
            flops=6 * slots * width * ff,
            bytes_accessed=6 * width * ff + 12 * blocks * rows * width,
            transcendentals=slots * ff,
        ),
        name="feed_first" if first else "feed_second",
    )(*operands, *waits)


def collect_near(own, by_x, by_y, from_a, from_b, *waits):
    half = from_a.shape[0]
    if waits:
        by_x, by_y = hold([by_x, by_y], *waits)
    by_y = jnp.concatenate([by_y[:half] + from_a, by_y[half:]])
    by_x = jnp.concatenate([by_x[:half], by_x[half:] + from_b])
    return own, swap_x(by_x), swap_y(by_y)


def add_up(parts):
    return sum(part.astype(jnp.float32) for part in parts)


def routing(ids, gates, expert_count, waits):
    dev_size = lax.axis_size("dev")
    planes = dev_size // 2
    named = ids.T[None] == jnp.arange(expert_count, dtype=jnp.int32)[:, None, None]
    [dense] = hold([jnp.sum(jnp.where(named, gates.T[None], 0.0), axis=1)], *waits)
    pair = jnp.stack([dense, swap_x(dense)])
    four = jnp.concatenate([pair, swap_y(pair)])
    every = jnp.stack([four] + [turn(four, k) for k in range(1, planes)])
    me = lax.axis_index("grp") * dev_size + lax.axis_index("dev")
    mine = jnp.stack(
        [lax.dynamic_index_in_dim(every, e, 2, keepdims=False) for e in (me, me ^ 1)], axis=1
    )
    named = mine > 0
    tokens = mine.shape[-1]
    before = jnp.triu(jnp.ones((tokens, tokens), jnp.bfloat16), 1)
    rank = jnp.dot(named.astype(jnp.bfloat16), before, preferred_element_type=jnp.float32)
    return jnp.where(named, rank, -1.0).astype(jnp.int32), mine, (pair, four)


def shards(
    queries,
    keys,
    values,
    doc_ids,
    out_weight,
    norm_gain,
    expert_ids,
    gate_values,
    expert_gate,
    expert_up,
    expert_down,
):
    own_rows = queries.shape[0]
    grp_size = lax.axis_size("grp")
    dev_size = lax.axis_size("dev")
    planes = dev_size // 2
    group, device = lax.axis_index("grp"), lax.axis_index("dev")
    dev_rows = own_rows // grp_size
    width = out_weight.shape[1]
    top_count = expert_ids.shape[2]
    expert_count = grp_size * dev_size
    capacity = max(2, 3 * dev_rows * top_count // (2 * expert_count))
    slots = -(-capacity // 16) * 16
    doc_reach = dev_size * own_rows // 2 + own_rows
    reach = min(dev_size - 1, (doc_reach + own_rows - 1) // own_rows)

    pieces = gather_keys(keys, values, reach)
    own_low = (len(pieces) - 2 + device % 2) * own_rows
    own_docs = lax.dynamic_slice_in_dim(doc_ids, device * own_rows, own_rows, 0)
    starts = jnp.sum((doc_ids[None, :] < own_docs[:, None]).astype(jnp.int32), axis=1)
    starts = starts - device * own_rows + own_low
    ends = jnp.stack([starts[::dev_rows], starts[dev_rows - 1 :: dev_rows]], axis=1)
    core = device % 2
    by_role = [group ^ (1 + core), group ^ (2 - core), group ^ 3, group]
    bounds = jnp.concatenate([jnp.stack([own_low, *by_role[:3], core, *by_role[3:]]), ends.reshape(-1)]).astype(jnp.int32)

    slot_of, gates, steps = routing(expert_ids[0], gate_values[0], expert_count, pieces[-2:])
    own_weights = [expert_gate[0], expert_up[0], expert_down[0]]
    other_weights = [swap_core(w) for w in own_weights]

    def part(role, *waits):
        attended = attend(role, queries, pieces, starts, bounds, dev_rows, waits)
        return jnp.dot(attended, out_weight, preferred_element_type=jnp.float32)

    half = dev_rows // 2
    far = part(3).astype(jnp.bfloat16)
    from_a, from_b = swap_x(far[:half]), swap_y(far[half:])
    by_x = part(1, far, steps[0]).astype(jnp.bfloat16)
    by_y = part(2, by_x, steps[1], *other_weights).astype(jnp.bfloat16)
    own = part(5, slot_of, gates, from_a, from_b)
    projected = add_up(collect_near(own, by_x, by_y, from_a, from_b))
    normed = (
        projected
        * lax.rsqrt(jnp.mean(projected * projected, axis=-1, keepdims=True) + 1e-06)
        * norm_gain
    ).astype(jnp.bfloat16)

    order = list(range(planes))
    turned = order[1:] + order[:1]
    sets = [turned[i : i + 2] for i in range(0, planes, 2)]
    blocks, done = {}, {}

    def feed_first(members, *waits):
        routes = [jnp.stack([part[k] for k in members]) for part in (slot_of, gates)]
        inputs = [b for k in members for b in blocks[k]]
        results = feed(True, inputs, *routes, slots, own_weights, [], dev_rows, waits)
        return members, routes, *results

    def feed_second(state, *waits):
        members, routes, given, other = state
        out = feed(False, [], *routes, slots, other_weights, [other, given], dev_rows, waits)
        for i, k in enumerate(members):
            done[k] = out[5 * i : 5 * i + 5]
        return out[0]

    def relay(near, *waits):
        first, second = halves(*near, *waits) if waits else (near[0][:half], near[1][half:])
        return swap_y(first), swap_x(second)

    near, sent, fars = (), [], [(), ()]

    def launch(k):
        nonlocal near
        block = normed
        if k:
            block = jnp.copy(normed)
            if len(sent) > 1:
                [block] = hold([block], *sent[-2])
            [block] = hold([turn(block, k)], *near, *fars[-2])
        near = swap_x(block), swap_y(block)
        blocks[k] = [block]

    def relay(k, *waits):
        nonlocal near
        near = hold(near, *waits) if waits else near
        sent.append((near[0][:half], near[1][half:]))
        far = swap_y(sent[-1][0]), swap_x(sent[-1][1])
        fars.append(far)
        blocks[k] += [*near, *far]
        return far

    launch(0)
    far = relay(0)
    for i, members in enumerate(sets[:-1]):
        for k in members:
            if k not in blocks:
                launch(k)
                relay(k)
        following = next(k for k in sets[i + 1] if k)
        state = feed_first(members)
        launch(following)
        far = relay(following, state[2])
        feed_second(state, *near)

    early = [k for members in sets[:-1][::-1] for k in members[::-1]]
    late = [k for k in sets[-1] if k] + [0]
    froms, sums = {}, []

    def far_part(k):
        froms[k] = swap_x(done[k][3]), swap_y(done[k][4])
        return froms[k]

    def near_part(k, *waits):
        parts = collect_near(*done[k][:3], *froms[k], *waits)
        summed = add_up(parts)
        if k:
            summed = turn(summed.astype(jnp.bfloat16), planes - k).astype(jnp.float32)
        sums.append(summed)
        return parts[1:]

    def held(k, *waits):
        done[k] = [*done[k][:3], *hold(done[k][3:5], *waits)]

    chain = far
    for k in early[:1]:
        held(k, *chain)
        chain = far_part(k)
    state = feed_first(sets[-1], *chain)
    arrived = ()
    for k in early[:1]:
        arrived = near_part(k)
    for k in early[1:]:
        held(k, *chain)
        chain = far_part(k)
    feed_second(state, *arrived, *chain)
    for k in early[1:]:
        arrived = near_part(k, state[2])
    chain = arrived
    for k in late:
        held(k, *chain)
        chain = far_part(k)
        near_part(k)
    return (projected + sum(sums)).astype(jnp.bfloat16)[None]


def solution(mesh):
    return jax.shard_map(
        shards,
        mesh=mesh,
        in_specs=(
            P("dev", "grp"),
            P("dev", "grp"),
            P("dev", "grp"),
            P(),
            P("grp", None),
            P(),
            P("dev", "grp", None),
            P("dev", "grp", None),
            P(("grp", "dev"), None, None),
            P(("grp", "dev"), None, None),
            P(("grp", "dev"), None, None),
        ),
        out_specs=P("dev", "grp", None),
        check_vma=False,
    )
```

```python
import functools
import math

import jax
import jax.numpy as jnp
from jax import lax
from jax.experimental import pallas as pl
from jax.experimental.pallas import tpu as pltpu
from jax.sharding import PartitionSpec as P

HEAD_SIZE = 128
KEY_BLOCK = 512
SPLIT = 8
IN_TILE = 768
OUT_TILE = 512
VMEM_BYTES = 56 * 1024 * 1024
LOW = -1e30


def after(value, *others):
    return lax.optimization_barrier((value, *others))[0]


def swap_x(value):
    return lax.ppermute(value, "grp", [(i, i ^ 1) for i in range(lax.axis_size("grp"))])


def swap_y(value):
    return lax.ppermute(value, "grp", [(i, i ^ 2) for i in range(lax.axis_size("grp"))])


def swap_core(value):
    return lax.ppermute(value, "dev", [(i, i ^ 1) for i in range(lax.axis_size("dev"))])


def turn(value, planes):
    count = lax.axis_size("dev")
    return lax.ppermute(value, "dev", [(i, (i - 2 * planes) % count) for i in range(count)])


def earlier(value, steps, sources=lambda source: True):
    count = lax.axis_size("dev")
    pairs = [(i, i + steps) for i in range(count - steps) if sources(i)]
    return lax.ppermute(value, "dev", pairs)


def hold_kernel(*refs):
    del refs


def hold(values, *waits):
    anywhere = pl.BlockSpec(memory_space=pl.ANY)
    return pl.pallas_call(
        hold_kernel,
        in_specs=[anywhere] * (len(values) + len(waits)),
        out_specs=[anywhere] * len(values),
        out_shape=[jax.ShapeDtypeStruct(v.shape, v.dtype) for v in values],
        input_output_aliases={i: i for i in range(len(values))},
        cost_estimate=pl.CostEstimate(flops=0, bytes_accessed=0, transcendentals=0),
        name="hold",
    )(*values, *waits)


def gather_keys(keys, values, reach):
    own = jnp.concatenate([keys, values], axis=1)
    whole = reach // 2
    lanes = [own]
    for _ in range(whole):
        lanes.append(earlier(lanes[-1], 2))
    pieces = [piece for lane in lanes[::-1] for piece in (lane, swap_core(lane))]
    if reach % 2:
        pieces = [earlier(own, reach, lambda source: source % 2 == 1)] + pieces
    return pieces


def attend_kernel(bounds, *refs, shards, waits, mask):
    q_ref, start_ref = refs[:2]
    pieces = refs[2 : 2 + shards]
    out_ref, q_all, kv_ref, top, total = refs[2 + shards + waits :]
    size = pieces[0].shape[0]
    core = bounds[2]
    for i, piece in enumerate(pieces):
        lone = shards % 2
        if i < lone:
            at = 0
        else:
            pair = i - (i - lone) % 2
            at = pair + (core if pair == i else 1 - core)
        kv_ref[pl.ds(pl.multiple_of(at * size, size), size), :] = piece[...]
    rows = q_ref.shape[0]
    heads = q_ref.shape[1] // HEAD_SIZE
    for h in range(heads):
        q_all[h * rows : (h + 1) * rows, :] = q_ref[:, h * HEAD_SIZE : (h + 1) * HEAD_SIZE]
    top[...] = jnp.full_like(top, LOW)
    total[...] = jnp.zeros_like(total)
    block_index = bounds[1] ^ mask
    q_low = bounds[0] + block_index * rows
    first_start, last_start = bounds[3 + 2 * block_index], bounds[4 + 2 * block_index]
    factor = math.log2(math.e) / math.sqrt(HEAD_SIZE)

    def step(block, masked):
        low = pl.multiple_of(block * KEY_BLOCK, KEY_BLOCK)
        key = kv_ref[pl.ds(low, KEY_BLOCK), :HEAD_SIZE]
        value = kv_ref[pl.ds(low, KEY_BLOCK), HEAD_SIZE:]
        value = jnp.concatenate([value, jnp.ones_like(value)], axis=1)
        if masked:
            key_pos = low + lax.broadcasted_iota(jnp.int32, (rows, KEY_BLOCK), 1)
            q_pos = q_low + lax.broadcasted_iota(jnp.int32, (rows, KEY_BLOCK), 0)
            seen = (key_pos >= start_ref[...]) & (key_pos <= q_pos)
        part_heads = heads // SPLIT
        size = part_heads * rows
        scores = []
        for r in range(SPLIT):
            scores.append(lax.dot_general(
                q_all[r * size : (r + 1) * size, :], key, (((1,), (1,)), ((), ())), preferred_element_type=jnp.float32
            ))
        for r in range(SPLIT):
            span = slice(r * size, (r + 1) * size)
            score = scores[r] * factor
            if masked:
                score = jnp.where(seen[None], score.reshape(part_heads, rows, KEY_BLOCK), LOW)
                score = score.reshape(size, KEY_BLOCK)
            old = top[span, :]
            new = jnp.maximum(old, jnp.max(score, axis=1, keepdims=True))
            weight = jnp.exp2(score - jnp.concatenate([new] * (KEY_BLOCK // HEAD_SIZE), axis=1))
            shrink = jnp.exp2(old - new)
            added = jnp.dot(weight.astype(jnp.bfloat16), value, preferred_element_type=jnp.float32)
            total[span, :] = total[span, :] * jnp.concatenate([shrink, shrink], axis=1) + added
            top[span, :] = new

    def loop(low, high, masked):
        def body(block, carry):
            step(block, masked)
            return carry

        lax.fori_loop(low, high, body, 0)

    begin = first_start // KEY_BLOCK
    end = (q_low + rows - 1) // KEY_BLOCK + 1
    inner_low = jnp.minimum((last_start + KEY_BLOCK - 1) // KEY_BLOCK, end)
    inner_high = jnp.maximum((q_low + 1) // KEY_BLOCK, inner_low)
    loop(begin, inner_low, True)
    loop(inner_low, inner_high, False)
    loop(inner_high, end, True)
    for h in range(heads):
        part = total[h * rows : (h + 1) * rows, :]
        out_ref[:, h * HEAD_SIZE : (h + 1) * HEAD_SIZE] = (
            part[:, :HEAD_SIZE] / part[:, HEAD_SIZE:]
        ).astype(out_ref.dtype)


def attend(mask, queries, pieces, starts, bounds, rows, waits=()):
    width = queries.shape[1]
    heads = width // HEAD_SIZE
    length = len(pieces) * pieces[0].shape[0]
    pairs = heads * rows * length // 2
    return pl.pallas_call(
        functools.partial(attend_kernel, shards=len(pieces), waits=len(waits), mask=mask),
        grid_spec=pltpu.PrefetchScalarGridSpec(
            num_scalar_prefetch=1,
            grid=(1,),
            in_specs=[
                pl.BlockSpec((rows, width), lambda i, bounds: (bounds[1] ^ mask, 0)),
                pl.BlockSpec((rows, 1), lambda i, bounds: (bounds[1] ^ mask, 0)),
            ]
            + [pl.BlockSpec(p.shape, lambda i, bounds: (0, 0)) for p in pieces]
            + [pl.BlockSpec(memory_space=pl.ANY)] * len(waits),
            out_specs=pl.BlockSpec((rows, width), lambda i, bounds: (0, 0)),
            scratch_shapes=[
                pltpu.VMEM((heads * rows, HEAD_SIZE), jnp.bfloat16),
                pltpu.VMEM((length, 2 * HEAD_SIZE), jnp.bfloat16),
                pltpu.VMEM((heads * rows, HEAD_SIZE), jnp.float32),
                pltpu.VMEM((heads * rows, 2 * HEAD_SIZE), jnp.float32),
            ],
        ),
        out_shape=jax.ShapeDtypeStruct((rows, width), jnp.bfloat16),
        compiler_params=pltpu.CompilerParams(vmem_limit_bytes=VMEM_BYTES),
        cost_estimate=pl.CostEstimate(
            flops=4 * pairs * HEAD_SIZE, bytes_accessed=4 * length * HEAD_SIZE, transcendentals=pairs
        ),
        name="attend",
    )(bounds, queries, starts[:, None], *pieces, *waits)


def feed_kernel(*refs, blocks, first, waits):
    refs = list(refs)
    gates_kept, hidden, gate_buf, up_buf, down_buf, sems = refs[-6:]
    del refs[-6:]
    incoming = [refs.pop(0) for _ in range(5 * blocks)] if first else None
    slot_of, gates, gate_ref, up_ref, down_ref = (refs.pop(0) for _ in range(5))
    if not first:
        taken, earlier_given = refs.pop(0), refs.pop(0)
    refs = refs[waits:]
    if first:
        given, other, taken = refs
    else:
        outgoing, given = refs[: 5 * blocks], refs[5 * blocks]
    loads = [
        pltpu.make_async_copy(source, target, sems.at[i])
        for i, (source, target) in enumerate(
            ((gate_ref, gate_buf), (up_ref, up_buf), (down_ref, down_buf))
        )
    ]
    for load in loads:
        load.start()
    tokens = slot_of.shape[3]
    half = tokens // 2
    slots = given.shape[0] // (2 * blocks)
    each = slots // 2

    def chosen(p, e, b):
        at = 2 * p + b
        mine = slot_of[at // 4, e, at % 4 : at % 4 + 1, :]
        return lax.broadcasted_iota(jnp.int32, (each, tokens), 0) == mine

    def pick(p):
        lines = []
        for e in range(2):
            for b in range(2):
                found = chosen(p, e, b).astype(jnp.float32)
                zeros = jnp.zeros_like(found)
                lines.append(jnp.concatenate([zeros, found] if b else [found, zeros], axis=1))
        return jnp.concatenate(lines).astype(jnp.bfloat16)

    def share(e):
        parts = []
        for p in range(2 * blocks):
            for b in range(2):
                at = 2 * p + b
                gate = gates[at // 4, e, at % 4 : at % 4 + 1, :]
                parts.append(jnp.sum(jnp.where(chosen(p, e, b), gate, 0.0), axis=1, keepdims=True))
        return jnp.concatenate(parts)

    if first:
        for p in range(2 * blocks):
            at = 5 * (p // 2) + 2 * (p % 2)
            held = jnp.concatenate([piece[...] for piece in incoming[at : at + 2 + p % 2]])
            found = jnp.dot(pick(p), held, preferred_element_type=jnp.float32).astype(taken.dtype)
            taken[p * slots : (p + 1) * slots, :] = found[:slots]
            other[p * slots : (p + 1) * slots, :] = found[slots:]

    ff, width = down_buf.shape
    inner, outer = math.gcd(ff, IN_TILE), math.gcd(width, OUT_TILE)

    def tiles(count, body):
        lax.fori_loop(0, count, lambda i, carry: (body(i), carry)[1], 0)

    def gate_tile(i):
        at = pl.ds(pl.multiple_of(i * inner, inner), inner)
        gate = jnp.dot(taken[...], gate_buf[:, at], preferred_element_type=jnp.float32)
        gates_kept[:, at] = gate / (1.0 + jnp.exp(-gate))

    def up_tile(i):
        at = pl.ds(pl.multiple_of(i * inner, inner), inner)
        up = jnp.dot(taken[...], up_buf[:, at], preferred_element_type=jnp.float32)
        hidden[:, at] = (gates_kept[:, at] * up).astype(jnp.bfloat16)

    def down_tile(i):
        at = pl.ds(pl.multiple_of(i * outer, outer), outer)
        part = jnp.dot(hidden[...], down_buf[:, at], preferred_element_type=jnp.float32)
        given[:, at] = (part * shares).astype(given.dtype)

    loads[0].wait()
    tiles(ff // inner, gate_tile)
    loads[1].wait()
    tiles(ff // inner, up_tile)
    shares = share(0 if first else 1)
    loads[2].wait()
    tiles(width // outer, down_tile)
    if not first:
        for p in range(2 * blocks):
            at = 5 * (p // 2) + 2 * (p % 2)
            place = slice(p * slots, (p + 1) * slots)
            rows = jnp.concatenate([earlier_given[place, :], given[place, :]])
            back = lax.dot_general(
                pick(p), rows, (((0,), (0,)), ((), ())), preferred_element_type=jnp.float32
            ).astype(jnp.bfloat16)
            outgoing[at][...] = back[:tokens]
            if p % 2 == 0:
                outgoing[at + 1][...] = back[tokens:]
            else:
                outgoing[at + 1][...] = back[tokens : tokens + half]
                outgoing[at + 2][...] = back[tokens + half :]


def feed(first, inputs, slot_of, gates, slots, weights, extra, rows, waits=()):
    width, ff = weights[0].shape
    blocks = slot_of.shape[0]
    slots = 4 * blocks * slots

    def whole(shape):
        return pl.BlockSpec(shape, lambda i: (0,) * len(shape))

    shapes = ([(rows, width)] * 3 + [(rows // 2, width), (rows - rows // 2, width)]) * blocks
    operands = [*inputs, slot_of, gates, *weights, *extra]
    specs = [whole(v.shape) for v in operands]
    at = len(inputs) + 2
    specs[at : at + 3] = [pl.BlockSpec(memory_space=pl.ANY)] * 3
    specs += [pl.BlockSpec(memory_space=pl.ANY)] * len(waits)
    results = [(slots, width)] * 2 if first else shapes
    kept = pltpu.VMEM((slots, width), jnp.bfloat16)
    return pl.pallas_call(
        functools.partial(feed_kernel, blocks=blocks, first=first, waits=len(waits)),
        grid=(1,),
        in_specs=specs,
        out_specs=[whole(s) for s in results],
        out_shape=[jax.ShapeDtypeStruct(s, jnp.bfloat16) for s in results],
        scratch_shapes=[
            kept,
            pltpu.VMEM((slots, ff), jnp.float32),
            pltpu.VMEM((slots, ff), jnp.bfloat16),
        ]
        + [pltpu.VMEM(w.shape, w.dtype) for w in weights]
        + [pltpu.SemaphoreType.DMA((3,))],
        compiler_params=pltpu.CompilerParams(vmem_limit_bytes=VMEM_BYTES),
        cost_estimate=pl.CostEstimate(
            flops=6 * slots * width * ff,
            bytes_accessed=6 * width * ff + 12 * blocks * rows * width,
            transcendentals=slots * ff,
        ),
        name="feed_first" if first else "feed_second",
    )(*operands, *waits)


def collect_near(own, by_x, by_y, from_a, from_b, *waits):
    half = from_a.shape[0]
    if waits:
        by_x, by_y = hold([by_x, by_y], *waits)
    by_y = jnp.concatenate([by_y[:half] + from_a, by_y[half:]])
    by_x = jnp.concatenate([by_x[:half], by_x[half:] + from_b])
    return own, swap_x(by_x), swap_y(by_y)


def add_up(parts):
    return sum(part.astype(jnp.float32) for part in parts)


def routing(ids, gates, expert_count, waits):
    dev_size = lax.axis_size("dev")
    planes = dev_size // 2
    named = ids.T[None] == jnp.arange(expert_count, dtype=jnp.int32)[:, None, None]
    [dense] = hold([jnp.sum(jnp.where(named, gates.T[None], 0.0), axis=1)], *waits)
    pair = jnp.stack([dense, swap_x(dense)])
    four = jnp.concatenate([pair, swap_y(pair)])
    every = jnp.stack([four] + [turn(four, k) for k in range(1, planes)])
    me = lax.axis_index("grp") * dev_size + lax.axis_index("dev")
    mine = jnp.stack(
        [lax.dynamic_index_in_dim(every, e, 2, keepdims=False) for e in (me, me ^ 1)], axis=1
    )
    named = mine > 0
    tokens = mine.shape[-1]
    before = jnp.triu(jnp.ones((tokens, tokens), jnp.bfloat16), 1)
    rank = jnp.dot(named.astype(jnp.bfloat16), before, preferred_element_type=jnp.float32)
    return jnp.where(named, rank, -1.0).astype(jnp.int32), mine, (pair, four)


def shards(
    queries,
    keys,
    values,
    doc_ids,
    out_weight,
    norm_gain,
    expert_ids,
    gate_values,
    expert_gate,
    expert_up,
    expert_down,
):
    own_rows = queries.shape[0]
    grp_size = lax.axis_size("grp")
    dev_size = lax.axis_size("dev")
    planes = dev_size // 2
    group, device = lax.axis_index("grp"), lax.axis_index("dev")
    dev_rows = own_rows // grp_size
    width = out_weight.shape[1]
    top_count = expert_ids.shape[2]
    expert_count = grp_size * dev_size
    capacity = max(2, 3 * dev_rows * top_count // (2 * expert_count))
    slots = -(-capacity // 16) * 16
    doc_reach = dev_size * own_rows // 2 + own_rows
    reach = min(dev_size - 1, (doc_reach + own_rows - 1) // own_rows)

    pieces = gather_keys(keys, values, reach)
    own_low = (len(pieces) - 2 + device % 2) * own_rows
    own_docs = lax.dynamic_slice_in_dim(doc_ids, device * own_rows, own_rows, 0)
    starts = jnp.sum((doc_ids[None, :] < own_docs[:, None]).astype(jnp.int32), axis=1)
    starts = starts - device * own_rows + own_low
    ends = jnp.stack([starts[::dev_rows], starts[dev_rows - 1 :: dev_rows]], axis=1)
    bounds = jnp.concatenate([jnp.stack([own_low, group, device % 2]), ends.reshape(-1)]).astype(jnp.int32)

    slot_of, gates, steps = routing(expert_ids[0], gate_values[0], expert_count, pieces[-2:])
    own_weights = [expert_gate[0], expert_up[0], expert_down[0]]
    other_weights = [swap_core(w) for w in own_weights]

    def part(mask, *waits):
        attended = attend(mask, queries, pieces, starts, bounds, dev_rows, waits)
        return jnp.dot(attended, out_weight, preferred_element_type=jnp.float32)

    half = dev_rows // 2
    far = part(3).astype(jnp.bfloat16)
    from_a, from_b = swap_x(far[:half]), swap_y(far[half:])
    by_x = part(1, far, steps[0]).astype(jnp.bfloat16)
    by_y = part(2, by_x, steps[1], *other_weights).astype(jnp.bfloat16)
    own = part(0, slot_of, gates, from_a, from_b)
    projected = add_up(collect_near(own, by_x, by_y, from_a, from_b))
    normed = (
        projected
        * lax.rsqrt(jnp.mean(projected * projected, axis=-1, keepdims=True) + 1e-06)
        * norm_gain
    ).astype(jnp.bfloat16)

    order = list(range(planes))
    turned = order[1:] + order[:1]
    sets = [turned[i : i + 2] for i in range(0, planes, 2)]
    blocks, done = {}, {}

    def feed_first(members, *waits):
        routes = [jnp.stack([part[k] for k in members]) for part in (slot_of, gates)]
        inputs = [b for k in members for b in blocks[k]]
        results = feed(True, inputs, *routes, slots, own_weights, [], dev_rows, waits)
        return members, routes, *results

    def feed_second(state, *waits):
        members, routes, given, other = state
        out = feed(False, [], *routes, slots, other_weights, [other, given], dev_rows, waits)
        for i, k in enumerate(members):
            done[k] = out[5 * i : 5 * i + 5]
        return out[0]

    def relay(near, *waits):
        first, second = halves(*near, *waits) if waits else (near[0][:half], near[1][half:])
        return swap_y(first), swap_x(second)

    near, sent, fars = (), [], [(), ()]

    def launch(k):
        nonlocal near
        block = normed
        if k:
            block = jnp.copy(normed)
            if len(sent) > 1:
                [block] = hold([block], *sent[-2])
            [block] = hold([turn(block, k)], *near, *fars[-2])
        near = swap_x(block), swap_y(block)
        blocks[k] = [block]

    def relay(k, *waits):
        nonlocal near
        near = hold(near, *waits) if waits else near
        sent.append((near[0][:half], near[1][half:]))
        far = swap_y(sent[-1][0]), swap_x(sent[-1][1])
        fars.append(far)
        blocks[k] += [*near, *far]
        return far

    launch(0)
    far = relay(0)
    for i, members in enumerate(sets[:-1]):
        for k in members:
            if k not in blocks:
                launch(k)
                relay(k)
        following = next(k for k in sets[i + 1] if k)
        state = feed_first(members)
        launch(following)
        far = relay(following, state[2])
        feed_second(state, *near)

    early = [k for members in sets[:-1][::-1] for k in members[::-1]]
    late = [k for k in sets[-1] if k] + [0]
    froms, sums = {}, []

    def far_part(k):
        froms[k] = swap_x(done[k][3]), swap_y(done[k][4])
        return froms[k]

    def near_part(k, *waits):
        parts = collect_near(*done[k][:3], *froms[k], *waits)
        summed = add_up(parts)
        if k:
            summed = turn(summed.astype(jnp.bfloat16), planes - k).astype(jnp.float32)
        sums.append(summed)
        return parts[1:]

    def held(k, *waits):
        done[k] = [*done[k][:3], *hold(done[k][3:5], *waits)]

    chain = far
    for k in early[:1]:
        held(k, *chain)
        chain = far_part(k)
    state = feed_first(sets[-1], *chain)
    arrived = ()
    for k in early[:1]:
        arrived = near_part(k)
    for k in early[1:]:
        held(k, *chain)
        chain = far_part(k)
    feed_second(state, *arrived, *chain)
    for k in early[1:]:
        arrived = near_part(k, state[2])
    chain = arrived
    for k in late:
        held(k, *chain)
        chain = far_part(k)
        near_part(k)
    return (projected + sum(sums)).astype(jnp.bfloat16)[None]


def solution(mesh):
    return jax.shard_map(
        shards,
        mesh=mesh,
        in_specs=(
            P("dev", "grp"),
            P("dev", "grp"),
            P("dev", "grp"),
            P(),
            P("grp", None),
            P(),
            P("dev", "grp", None),
            P("dev", "grp", None),
            P(("grp", "dev"), None, None),
            P(("grp", "dev"), None, None),
            P(("grp", "dev"), None, None),
        ),
        out_specs=P("dev", "grp", None),
        check_vma=False,
    )
```
